32 devices in a mesh: groups: 2 (over y), dp: 4 (over z), tensor: 2 (over x), sub: 2 (over core).
Axes of the slice: x: 2, y: 2, z: 4, core: 2. Of those that a mesh axis runs over, the one named last changes fastest.
Arguments:
- tokens: bfloat16 [5120, 16384], P(('groups', 'dp', 'sub'), 'tensor'), parts along dimension 0, may hold values from -6 to 6
- gate_weight: bfloat16 [1664, 16384], P(('dp', 'sub'), 'tensor'), may hold values from -0.046875 to 0.046875
- up_weight: bfloat16 [1664, 16384], P(('dp', 'sub'), 'tensor'), may hold values from -0.046875 to 0.046875
- down_weight: bfloat16 [1664, 16384], P(('dp', 'sub'), 'tensor'), may hold values from -0.21875 to 0.21875
Outputs:
- ffn_out: bfloat16 [5120, 16384], P(('groups', 'dp', 'sub'), 'tensor'), parts along dimension 0
The draws below stay inside these ranges and needn't reach their ends.
There are 2 independent parts, one for each index of `groups`. The reference program is written for one: setup_inputs(seed, part) draws one part's arguments, and reference() takes and returns one part's arrays. A program takes and returns all parts, laid end to end along the dimension named above; an argument that names none is the same for every part. Nothing has to cross between parts.
All inputs are finite; a program needn't handle non-finite values.
Results may differ from the reference program's by a relative error of at most 0.014.
Values may be sent and summed in bfloat16 or wider, within the bound.
No kernel may reach another device: no remote copies, remote signals or barrier semaphores. Data moves between devices by JAX's collectives and lax.ppermute only.
A program may use at most 192 MiB of HBM per device.

```python
import jax
import jax.numpy as jnp
from jax import lax

D = 16384
HC = 208
STEPS = 2
ROWS = 320
TOKENS = 2560
HIDDEN_SIZE = 1664
MET = 832
N_DP = 4
N_TENSOR = 2
N_SUB = 2


def block_levels(key, shape, split, smallest, top_value):
    level = 1.0
    for axis_at, shards_of in split:
        steps = jax.random.uniform(jax.random.fold_in(jax.random.fold_in(key, 6), axis_at), (shards_of,), jnp.float32, smallest / len(split), top_value / len(split))
        level = level * jnp.repeat(jnp.exp(steps), shape[axis_at] // shards_of).reshape((-1,) + (1,) * (len(shape) - 1 - axis_at))
    return level


def gaussian(own_key, shape, scale, limit, cuts=(), kind=jnp.bfloat16):
    array = jax.random.normal(own_key, shape, jnp.float32) * scale
    if len(cuts) > 0:
        array = block_levels(own_key, shape, cuts, -0.22, 0.18) * array
    return jnp.clip(array, min=-limit, max=limit).astype(kind)


def setup_inputs(seed: int = 0, part: int = 0) -> dict:
    streams_of = jax.random.split(jax.random.key(seed), 5)
    part_keys = jax.random.split(jax.random.fold_in(streams_of[4], part), 5)
    tokens = gaussian(part_keys[0], (TOKENS, D), 1.0, 6.0, ((0, 8), (1, 2)))
    gate_weight = gaussian(streams_of[1], (HIDDEN_SIZE, D), D ** -0.5, 0.046875, ((0, 8), (1, 2)))
    up_weight = gaussian(streams_of[2], (HIDDEN_SIZE, D), D ** -0.5, 0.046875, ((0, 8), (1, 2)))
    down_weight = gaussian(streams_of[3], (HIDDEN_SIZE, D), MET ** -0.5, 0.21875, ((0, 8), (1, 2)))
    return dict(tokens=tokens, gate_weight=gate_weight, up_weight=up_weight, down_weight=down_weight)


def reference(tokens, gate_weight, up_weight, down_weight):
    row_block = ROWS * N_SUB
    span = HC * N_SUB
    width = D // N_TENSOR

    def one_block(index):
        rows = lax.dynamic_slice_in_dim(tokens, (index * row_block).astype(jnp.int32), row_block, 0)
        total = jnp.zeros((row_block, D), jnp.float32)
        for step in range(STEPS):
            source = jnp.mod(index - step + N_DP, N_DP).astype(jnp.int32)
            start = (source * span).astype(jnp.int32)
            gate_rows = lax.dynamic_slice_in_dim(gate_weight, start, span, 0)
            up_rows = lax.dynamic_slice_in_dim(up_weight, start, span, 0)
            down_rows = lax.dynamic_slice_in_dim(down_weight, start, span, 0)
            summed = jnp.zeros((row_block, 2 * span), jnp.float32)
            for slot in range(N_TENSOR):
                lo = slot * width
                piece = rows[:, lo:lo + width]
                both = jnp.concatenate([gate_rows[:, lo:lo + width], up_rows[:, lo:lo + width]], axis=0)
                partial_value = jnp.dot(piece, both.T, preferred_element_type=jnp.float32).astype(jnp.bfloat16)
                partial_value = lax.optimization_barrier(partial_value)
                summed = summed + partial_value.astype(jnp.float32)
            hidden = (jax.nn.silu(summed[:, :span]) * summed[:, span:]).astype(jnp.bfloat16)
            total = total + jnp.dot(hidden, down_rows, preferred_element_type=jnp.float32)
        return total.astype(jnp.bfloat16)

    blocks = lax.map(one_block, jnp.arange(N_DP, dtype=jnp.int32))
    return blocks.reshape(N_DP * row_block, D)
```

```python
import jax
import jax.numpy as jnp
from jax import lax
from jax.sharding import PartitionSpec as P

ROW_PARTS = 4
LANE_PARTS = 4


def shifted(block, axis, distance):
    devices = range(lax.axis_size(axis))
    route = [((i - distance) % len(devices), i) for i in devices]
    return lax.ppermute(block, axis, route)


def cuts(total, unit, parts):
    units = total // unit
    marks = [units * i // parts * unit for i in range(parts)] + [total]
    return list(zip(marks[:-1], marks[1:]))


def by_features(rows, units):
    return lax.dot_general(
        rows, units, (((1,), (1,)), ((), ())), preferred_element_type=jnp.float32
    )


def partial_values(row_sets, unit_sets):
    return jnp.concatenate(
        [
            jnp.concatenate([by_features(r, u) for u in unit_sets], axis=1)
            for r in row_sets
        ],
        axis=0,
    ).astype(jnp.bfloat16)


def over_slices(partial_value):
    total = partial_value.astype(jnp.float32)
    for distance in range(1, lax.axis_size("tensor")):
        total = total + shifted(partial_value, "tensor", distance).astype(jnp.float32)
    return total


def gated(gate, up):
    return (jax.nn.silu(gate) * up).astype(jnp.bfloat16)


def on_device(tokens, gate_weight, up_weight, down_weight):
    units, width = gate_weight.shape
    rows = tokens.shape[0]
    first = lax.axis_index("groups") == 0

    def mate(block):
        return shifted(block, "sub", 1)

    def across(block):
        return shifted(block, "groups", 1)

    def in_order(own, other, axis):
        return jnp.where(
            first,
            jnp.concatenate([own, other], axis=axis),
            jnp.concatenate([other, own], axis=axis),
        )

    row_cuts = cuts(units, 16, ROW_PARTS)
    lane_cuts = cuts(width, 256, LANE_PARTS)
    pieces = [jnp.where(first, gate_weight[a:b], up_weight[a:b]) for a, b in row_cuts]
    for a, b in lane_cuts:
        mid = (a + b) // 2
        pieces.append(jnp.where(first, down_weight[:, a:mid], down_weight[:, mid:b]))

    landed = []
    for i, piece in enumerate(pieces):
        if i >= 2:
            piece, landed[i - 2] = lax.optimization_barrier((piece, landed[i - 2]))
        landed.append(shifted(piece, "dp", 1))
    crossed = [across(block) for block in landed]

    both_rows = [tokens, mate(tokens)]
    down_mate = mate(down_weight)

    here = over_slices(partial_values(both_rows, [gate_weight, up_weight]))
    here = gated(here[:, :units], here[:, units:])
    here = [here[:rows], mate(here[rows:])]

    there = []
    for i, (a, b) in enumerate(row_cuts):
        pre = over_slices(partial_values(both_rows, [landed[i], crossed[i]]))
        left, right = pre[:, : b - a], pre[:, b - a :]
        there.append(gated(jnp.where(first, left, right), jnp.where(first, right, left)))
    there = jnp.concatenate(there, axis=1)
    there = [there[:rows], mate(there[rows:])]

    results = []
    for i, (a, b) in enumerate(lane_cuts):
        own, other = landed[len(row_cuts) + i], crossed[len(row_cuts) + i]
        arrived = in_order(own, other, 1)
        arrived_mate = in_order(mate(own), mate(other), 1)
        total = jnp.zeros((rows, b - a), jnp.float32)
        for hidden, weight in (
            (here[0], down_weight[:, a:b]),
            (here[1], down_mate[:, a:b]),
            (there[0], arrived),
            (there[1], arrived_mate),
        ):
            total = total + jnp.dot(hidden, weight, preferred_element_type=jnp.float32)
        results.append(total.astype(jnp.bfloat16))
    return jnp.concatenate(results, axis=1)


def solution(mesh):
    return jax.shard_map(
        on_device,
        mesh=mesh,
        in_specs=(
            P(("groups", "dp", "sub"), "tensor"),
            P(("dp", "sub"), "tensor"),
            P(("dp", "sub"), "tensor"),
            P(("dp", "sub"), "tensor"),
        ),
        out_specs=P(("groups", "dp", "sub"), "tensor"),
        check_vma=False,
    )
```

```python
import functools

import jax
import jax.numpy as jnp
from jax import lax
from jax.experimental import pallas as pl
from jax.experimental.pallas import tpu as pltpu
from jax.sharding import PartitionSpec as P

ROW_SHARES = (1, 2, 2, 2, 2, 2, 2)
FIRST_BATCH = 4
LANE_SHARES = (3, 3, 3, 3, 2, 2)
VMEM = 24 * 1024 * 1024


def shifted(block, axis, distance):
    devices = range(lax.axis_size(axis))
    route = [((i - distance) % len(devices), i) for i in devices]
    return lax.ppermute(block, axis, route)


def tied(value, *earlier):
    return lax.optimization_barrier((value, *earlier))[0]


def cuts(total, unit, shares):
    units, whole, done, marks = total // unit, sum(shares), 0, [0]
    for share in shares:
        done += share
        marks.append(units * done // whole * unit)
    marks[-1] = total
    return list(zip(marks[:-1], marks[1:]))


def products_kernel(sets, *refs):
    row_refs, unit_refs, (out_ref, total) = refs[:sets], refs[sets:-2], refs[-2:]
    step = pl.program_id(0)

    @pl.when(step == 0)
    def _():
        total[...] = jnp.zeros_like(total)

    units = jnp.concatenate([ref[...] for ref in unit_refs], axis=0)
    rows = row_refs[0].shape[0]
    for i, ref in enumerate(row_refs):
        total[i * rows : (i + 1) * rows] += lax.dot_general(
            ref[...], units, (((1,), (1,)), ((), ())), preferred_element_type=jnp.float32
        )

    @pl.when(step == pl.num_programs(0) - 1)
    def _():
        out_ref[...] = total[...].astype(out_ref.dtype)


def products(row_sets, unit_sets):
    width = row_sets[0].shape[1]
    block = 1024 if width % 1024 == 0 else width
    count = sum(u.shape[0] for u in unit_sets)
    shape = (sum(r.shape[0] for r in row_sets), count)
    return pl.pallas_call(
        functools.partial(products_kernel, len(row_sets)),
        grid=(width // block,),
        in_specs=[
            pl.BlockSpec((array.shape[0], block), lambda k: (0, k))
            for array in (*row_sets, *unit_sets)
        ],
        out_specs=pl.BlockSpec(shape, lambda k: (0, 0)),
        out_shape=jax.ShapeDtypeStruct(shape, jnp.bfloat16),
        scratch_shapes=[pltpu.VMEM(shape, jnp.float32)],
        compiler_params=pltpu.CompilerParams(vmem_limit_bytes=VMEM),
        cost_estimate=pl.CostEstimate(flops=1, bytes_accessed=1, transcendentals=0),
    )(*row_sets, *unit_sets)


def output_kernel(a, b, side_ref, *refs):
    hidden, arrived, (down, down_mate) = refs[:4], refs[4:8], refs[8:10]
    out, here, here_mate, block, sems = refs[-5:]
    lanes = slice(a, b)
    copies = [
        pltpu.make_async_copy(down.at[:, lanes], here, sems.at[0]),
        pltpu.make_async_copy(down_mate.at[:, lanes], here_mate, sems.at[1]),
    ]
    for copy in copies:
        copy.start()
    half = (b - a) // 2
    side = side_ref[0]
    for copy in copies:
        copy.wait()
    for i in range(2):
        at = pl.ds(pl.multiple_of((side + i - 2 * side * i) * half, 128), half)
        total = None
        for rows, units in (
            (hidden[0], here[:, at]),
            (hidden[1], here_mate[:, at]),
            (hidden[2], arrived[i][...]),
            (hidden[3], arrived[2 + i][...]),
        ):
            term = jnp.dot(rows[...], units, preferred_element_type=jnp.float32)
            total = term if total is None else total + term
        block[:, at] = total.astype(block.dtype)
    copy = pltpu.make_async_copy(block, out.at[:, lanes], sems.at[2])
    copy.start()
    copy.wait()


def output_part(result, a, b, side, hidden, arrived, down, down_mate):
    rows, units, width = hidden[0].shape[0], down.shape[0], down.shape[1]
    any_space = pl.BlockSpec(memory_space=pl.ANY)
    whole = pl.BlockSpec(memory_space=pltpu.VMEM)
    operands = [side, *hidden, *arrived, down, down_mate]
    in_specs = [pl.BlockSpec(memory_space=pltpu.SMEM)] + [whole] * 8 + [any_space] * 2
    aliases = {}
    if result is not None:
        aliases = {len(operands): 0}
        operands.append(result)
        in_specs.append(any_space)
    return pl.pallas_call(
        functools.partial(output_kernel, a, b),
        in_specs=in_specs,
        out_specs=any_space,
        out_shape=jax.ShapeDtypeStruct((rows, width), jnp.bfloat16),
        scratch_shapes=[
            pltpu.VMEM((units, b - a), jnp.bfloat16),
            pltpu.VMEM((units, b - a), jnp.bfloat16),
            pltpu.VMEM((rows, b - a), jnp.bfloat16),
            pltpu.SemaphoreType.DMA((3,)),
        ],
        input_output_aliases=aliases,
        compiler_params=pltpu.CompilerParams(vmem_limit_bytes=VMEM),
        cost_estimate=pl.CostEstimate(flops=1, bytes_accessed=1, transcendentals=0),
    )(*operands)


def over_slices(partial_value):
    return [
        shifted(partial_value, "tensor", distance)
        for distance in range(1, lax.axis_size("tensor"))
    ]


def summed(partial_value, sent):
    total = partial_value.astype(jnp.float32)
    for block in sent:
        total = total + block.astype(jnp.float32)
    return total


def gated(gate, up):
    return (jax.nn.silu(gate) * up).astype(jnp.bfloat16)


def on_device(tokens, gate_weight, up_weight, down_weight):
    units, width = gate_weight.shape
    rows = tokens.shape[0]
    group = lax.axis_index("groups").astype(jnp.int32)
    first = group == 0
    side = group.reshape(1)

    def mate(block):
        return shifted(block, "sub", 1)

    row_cuts = cuts(units, 16, ROW_SHARES)
    lane_cuts = [(2 * a, 2 * b) for a, b in cuts(width // 2, 128, LANE_SHARES)]
    count = len(row_cuts)
    total_count = count + len(lane_cuts)

    def piece(i, *after):
        if i < count:
            a, b = row_cuts[i]
            gate, up = gate_weight, up_weight
            if after:
                gate, up = lax.optimization_barrier((gate, up, *after))[:2]
            return jnp.where(first, gate[a:b], up[a:b])
        a, b = lane_cuts[i - count]
        mid = (a + b) // 2
        down = tied(down_weight, *after) if after else down_weight
        return jnp.where(first, down[:, a:mid], down[:, mid:b])

    pieces = [piece(0)]
    pieces.append(piece(1, pieces[0]))
    pieces += [piece(i, pieces[1]) for i in range(2, total_count)]
    waiting = [shifted(pieces[0], "dp", 1), shifted(pieces[1], "dp", 1)]
    landed, crossed, mates, crossed_mates = [], [], {}, {}

    def advance(*after):
        i = len(landed)
        held = list(after)
        if i >= 1:
            held.append(landed[i - 1])
        if i >= 2:
            held.append(crossed[i - 2])
            if i - 2 >= count:
                held.append(mates[i - 2])
        if i - 3 >= count:
            held.append(crossed_mates[i - 3])
        block = tied(waiting[i], *held) if held else waiting[i]
        landed.append(block)
        crossed.append(shifted(block, "groups", 1))
        if i >= count:
            mates[i] = mate(block)
        if i - 2 >= count:
            crossed_mates[i - 2] = mate(tied(crossed[i - 2], block))
        if i + 2 < total_count:
            waiting.append(shifted(tied(pieces[i + 2], block), "dp", 1))
        return block

    def local(partial_value, sent, now):
        pre = summed(partial_value, [tied(block, now) for block in sent])
        return gated(pre[:, :units], pre[:, units:])

    def batch(lo, hi, now):
        held = lax.optimization_barrier((*landed[lo:hi], *crossed[lo:hi], now))[:-1]
        value = products([tokens, tokens_mate], held)
        return value, over_slices(value)

    def activated(partial_value, sent, now):
        pre = summed(partial_value, [tied(block, now) for block in sent])
        half = pre.shape[1] // 2
        left, right = pre[:, :half], pre[:, half:]
        return gated(jnp.where(first, left, right), jnp.where(first, right, left))

    tokens_mate = mate(tokens)
    down_mate = mate(tied(down_weight, pieces[0]))
    mine = products([tokens], [gate_weight, up_weight])
    mine_sent = over_slices(mine)
    now = advance(mine)
    theirs = products([tied(tokens_mate, now)], [gate_weight, up_weight])
    theirs_sent = over_slices(theirs)
    now = advance(theirs)
    here = local(mine, mine_sent, now)
    now = advance(here)
    here_mate = mate(local(theirs, theirs_sent, now))
    now = advance()
    now = advance(here_mate, down_mate)
    now = advance()
    early, early_sent = batch(0, FIRST_BATCH, now)
    now = advance(early)
    there = [activated(early, early_sent, now)]
    now = advance(there[0])
    now = advance()
    late, late_sent = batch(FIRST_BATCH, count, now)
    now = advance(late)
    there.append(activated(late, late_sent, now))
    there = jnp.concatenate(there, axis=1)
    there_mate = mate(there[rows:])
    there = there[:rows]
    now = advance(there)
    now = advance(there_mate)
    while len(landed) < total_count:
        now = advance()

    result = None
    for i, (a, b) in enumerate(lane_cuts):
        k = count + i
        if k not in crossed_mates:
            crossed_mates[k] = mate(crossed[k])
        result = output_part(
            result,
            a,
            b,
            side,
            [here, here_mate, there, there_mate],
            [landed[k], crossed[k], mates[k], crossed_mates[k]],
            down_weight,
            down_mate,
        )
    return result


def solution(mesh):
    return jax.shard_map(
        on_device,
        mesh=mesh,
        in_specs=(
            P(("groups", "dp", "sub"), "tensor"),
            P(("dp", "sub"), "tensor"),
            P(("dp", "sub"), "tensor"),
            P(("dp", "sub"), "tensor"),
        ),
        out_specs=P(("groups", "dp", "sub"), "tensor"),
        check_vma=False,
    )
```

```python
import functools

import jax
import jax.numpy as jnp
from jax import lax
from jax.experimental import pallas as pl
from jax.experimental.pallas import tpu as pltpu
from jax.sharding import PartitionSpec as P

GATE_SHARES = (6, 7)
UP_SHARES = (6, 7)
LANE_SHARES = (5, 5, 3, 2, 1)
VMEM = 24 * 1024 * 1024
CHEAP = pl.CostEstimate(flops=1, bytes_accessed=1, transcendentals=0)


def shifted(block, axis, distance):
    devices = range(lax.axis_size(axis))
    route = [((i - distance) % len(devices), i) for i in devices]
    return lax.ppermute(block, axis, route)


def mate(block):
    return shifted(block, "sub", 1)


def across(block):
    return shifted(block, "groups", 1)


def tied(value, *earlier):
    earlier = [e for e in earlier if e is not None]
    return lax.optimization_barrier((value, *earlier))[0] if earlier else value


def cuts(total, unit, shares):
    units, whole, done, marks = total // unit, sum(shares), 0, [0]
    for share in shares:
        done += share
        marks.append(units * done // whole * unit)
    marks[-1] = total
    return list(zip(marks[:-1], marks[1:]))


def by_features(rows, units):
    return lax.dot_general(
        rows, units, (((1,), (1,)), ((), ())), preferred_element_type=jnp.float32
    )


def products_kernel(sets, outs, block, steps, side_ref, *refs):
    count = len(refs) - len(outs) - 1
    operands, out_refs, total = refs[:count], refs[count:-1], refs[-1]
    side = side_ref[0]
    total[...] = jnp.zeros_like(total)

    def body(*blocks):
        units = jnp.concatenate([ref[...] for ref in blocks[len(sets) :]], axis=0)
        at = 0
        for ref in blocks[: len(sets)]:
            rows = ref.shape[0]
            total[at : at + rows] += by_features(ref[...], units)
            at += rows

    pltpu.emit_pipeline(
        body,
        grid=(steps,),
        in_specs=[
            pl.BlockSpec(
                (ref.shape[0], block),
                (lambda k: (0, side * steps + k))
                if i < len(sets) and sets[i]
                else (lambda k: (0, k)),
            )
            for i, ref in enumerate(operands)
        ],
    )(*operands)
    at = 0
    for out_ref in out_refs:
        rows = out_ref.shape[0]
        out_ref[...] = total[at : at + rows].astype(out_ref.dtype)
        at += rows


def products(side, row_sets, halved, unit_sets, out_types):
    width = unit_sets[0].shape[1]
    block = 1024 if width % 1024 == 0 else width
    count = sum(u.shape[0] for u in unit_sets)
    rows = sum(r.shape[0] for r in row_sets)
    part = rows // len(out_types)
    operands = (*row_sets, *unit_sets)
    return pl.pallas_call(
        functools.partial(
            products_kernel, halved, out_types, block, width // block
        ),
        in_specs=[pl.BlockSpec(memory_space=pltpu.SMEM)]
        + [pl.BlockSpec(memory_space=pltpu.HBM)] * len(operands),
        out_specs=[pl.BlockSpec(memory_space=pltpu.VMEM)] * len(out_types),
        out_shape=[jax.ShapeDtypeStruct((part, count), t) for t in out_types],
        scratch_shapes=[pltpu.VMEM((rows, count), jnp.float32)],
        compiler_params=pltpu.CompilerParams(vmem_limit_bytes=VMEM),
        cost_estimate=CHEAP,
    )(side, *operands)


def output_kernel(parts, side_ref, *refs):
    hidden, (down, down_mate) = refs[:4], refs[4:6]
    arrived = refs[6 : 6 + 4 * len(parts)]
    out, here, here_mate, block, sems = refs[-5:]
    side = side_ref[0]
    loads, stores, at = [], [], 0
    for i, (a, b, _) in enumerate(parts):
        spot = pl.ds(at, b - a)
        loads.append(
            [
                pltpu.make_async_copy(down.at[:, a:b], here.at[:, spot], sems.at[i, 0]),
                pltpu.make_async_copy(
                    down_mate.at[:, a:b], here_mate.at[:, spot], sems.at[i, 1]
                ),
            ]
        )
        stores.append(
            pltpu.make_async_copy(block.at[:, spot], out.at[:, a:b], sems.at[i, 2])
        )
        at += b - a
    for pair in loads:
        for copy in pair:
            copy.start()
    at = 0
    for i, (a, b, whole) in enumerate(parts):
        for copy in loads[i]:
            copy.wait()
        half = (b - a) // 2
        for j in range(2):
            where = (j if whole else side + j - 2 * side * j) * half
            lanes = pl.ds(pl.multiple_of(at + where, 128), half)
            sources = arrived[4 * i : 4 * i + 4]
            if whole:
                own = sources[0][:, j * half : (j + 1) * half]
                own_mate = sources[2][:, j * half : (j + 1) * half]
            else:
                own, own_mate = sources[j][...], sources[2 + j][...]
            total = None
            for rows, units in (
                (hidden[0], here[:, lanes]),
                (hidden[1], here_mate[:, lanes]),
                (hidden[2], own),
                (hidden[3], own_mate),
            ):
                term = jnp.dot(rows[...], units, preferred_element_type=jnp.float32)
                total = term if total is None else total + term
            block[:, lanes] = total.astype(block.dtype)
        stores[i].start()
        at += b - a
    for copy in stores:
        copy.wait()


def output_part(result, parts, side, hidden, arrived, down, down_mate):
    rows, units, width = hidden[0].shape[0], down.shape[0], down.shape[1]
    lanes = sum(b - a for a, b, _ in parts)
    any_space = pl.BlockSpec(memory_space=pl.ANY)
    whole = pl.BlockSpec(memory_space=pltpu.VMEM)
    operands = [side, *hidden, down, down_mate, *arrived]
    in_specs = (
        [pl.BlockSpec(memory_space=pltpu.SMEM)]
        + [whole] * 4
        + [any_space] * 2
        + [whole] * len(arrived)
    )
    aliases = {}
    if result is not None:
        aliases = {len(operands): 0}
        operands.append(result)
        in_specs.append(any_space)
    return pl.pallas_call(
        functools.partial(output_kernel, parts),
        in_specs=in_specs,
        out_specs=any_space,
        out_shape=jax.ShapeDtypeStruct((rows, width), jnp.bfloat16),
        scratch_shapes=[
            pltpu.VMEM((units, lanes), jnp.bfloat16),
            pltpu.VMEM((units, lanes), jnp.bfloat16),
            pltpu.VMEM((rows, lanes), jnp.bfloat16),
            pltpu.SemaphoreType.DMA((len(parts), 3)),
        ],
        input_output_aliases=aliases,
        compiler_params=pltpu.CompilerParams(vmem_limit_bytes=VMEM),
        cost_estimate=CHEAP,
    )(*operands)


def over_slices(partial_value):
    return [
        shifted(partial_value, "tensor", distance)
        for distance in range(1, lax.axis_size("tensor"))
    ]


def summed(partial_value, sent):
    total = partial_value.astype(jnp.float32)
    for block in sent:
        total = total + block.astype(jnp.float32)
    return total


def gated(gate, up):
    return (jax.nn.silu(gate) * up).astype(jnp.bfloat16)


def on_device(tokens, gate_weight, up_weight, down_weight):
    units, width = gate_weight.shape
    rows = tokens.shape[0]
    half = width // 2
    group = lax.axis_index("groups").astype(jnp.int32)
    side = group.reshape(1)

    def own_half(array, a, b):
        return lax.dynamic_slice(array, (a, group * half), (b - a, half))

    lane_cuts = [(2 * a, 2 * b) for a, b in cuts(half, 128, LANE_SHARES)]
    last = len(lane_cuts) - 1

    def down_piece(i):
        a, b = lane_cuts[i]
        if i == last:
            return down_later[:, a:b]
        return lax.dynamic_slice(
            down_later, (0, a + group * ((b - a) // 2)), (units, (b - a) // 2)
        )

    gate_cuts, up_cuts = cuts(units, 16, GATE_SHARES), cuts(units, 16, UP_SHARES)
    first = own_half(gate_weight, *gate_cuts[0])
    second = own_half(tied(gate_weight, first), *gate_cuts[1])
    swapped = lax.dynamic_slice(
        tied(tokens, second), (0, (1 - group) * half), (rows, half)
    )
    tokens_later, up_later, down_later = (
        tied(array, swapped) for array in (tokens, up_weight, down_weight)
    )
    pieces = [first, second]
    pieces += [own_half(up_later, a, b) for a, b in up_cuts]
    pieces += [down_piece(i) for i in range(len(lane_cuts))]
    base = len(pieces) - len(lane_cuts)

    waiting = [shifted(piece, "dp", 1) for piece in pieces[:2]]
    landed = []

    def take(*after):
        i = len(landed)
        landed.append(tied(waiting[i], *landed[-1:], *after))
        if i + 2 < len(pieces):
            waiting.append(shifted(tied(pieces[i + 2], landed[i]), "dp", 1))
        return landed[i]

    tokens_other = across(swapped)
    weights = [gate_weight, up_later]
    weights += [mate(weight) for weight in weights]
    down_mate = mate(down_later)

    def joint(unit_sets, *after):
        return products(
            side,
            [tokens_later, tokens_other],
            [True, False],
            [tied(u, *after) for u in unit_sets],
            [jnp.float32, jnp.bfloat16],
        )

    def one_slice(kept, given, *after):
        return (kept + tied(given, *after).astype(jnp.float32)).astype(jnp.bfloat16)

    own, other, own_mate, other_mate = {}, {}, {}, {}

    def spread(i, block):
        own[i] = block
        own_mate[i] = mate(block)
        if i < last:
            other[i] = across(block)

    def pass_on(i, *after):
        other[i] = tied(other[i], *after)
        other_mate[i] = mate(other[i])
        return other[i]

    def activated(pre):
        parts = [pre[:, i * units : (i + 1) * units] for i in range(4)]
        return gated(parts[0], parts[1]), gated(parts[2], parts[3])

    now = take()
    gate_a, gate_a_mate = now, mate(now)
    (mine,) = products(
        side, [tied(tokens_later, now)], [False], weights, [jnp.bfloat16]
    )
    mine_sent = over_slices(mine)

    now = take(mine)
    gate_b, gate_b_mate = now, mate(now)
    here, here_mate = activated(summed(mine, [tied(block, now) for block in mine_sent]))

    now = take(here, here_mate)
    up_a, up_a_mate = now, mate(now)
    tokens_other = tied(tokens_other, now)
    kept_a, sent_a = joint([gate_a, gate_b, gate_a_mate, gate_b_mate], tokens_other)
    given_a = across(sent_a)

    now = take(sent_a)
    kept_b, sent_b = joint([up_a, now, up_a_mate, mate(now)], now)
    given_b = across(sent_b)
    part_a = one_slice(kept_a, given_a, sent_b)
    slices_a = over_slices(part_a)

    now = take(part_a)
    spread(0, now)
    part_b = one_slice(kept_b, given_b, now)
    slices_b = over_slices(part_b)

    now = take(part_b)
    spread(1, now)
    gate_pre = summed(part_a, [tied(block, now) for block in slices_a])
    up_pre = summed(part_b, [tied(block, now) for block in slices_b])
    there = gated(gate_pre[:, :units], up_pre[:, :units])
    there_mate = gated(gate_pre[:, units:], up_pre[:, units:])
    now = pass_on(0, there, there_mate)

    now = take(now)
    spread(2, now)
    now = pass_on(1, now, down_mate)

    hidden = [here, here_mate, there, there_mate]

    def write(result, *which):
        parts, arrived = [], []
        for i in which:
            a, b = lane_cuts[i]
            whole = i == last
            parts.append((a, b, whole))
            arrived += (
                [own[i], own[i], own_mate[i], own_mate[i]]
                if whole
                else [own[i], other[i], own_mate[i], other_mate[i]]
            )
        return output_part(
            result, tuple(parts), side, hidden, arrived, down_weight, down_mate
        )

    result = write(None, 0, 1)
    now = take(now, result)
    spread(3, now)
    now = pass_on(2, now)
    now = take(now)
    spread(4, now)
    pass_on(3, now)
    result = write(result, 2)
    return write(result, 3, 4)


def solution(mesh):
    return jax.shard_map(
        on_device,
        mesh=mesh,
        in_specs=(
            P(("groups", "dp", "sub"), "tensor"),
            P(("dp", "sub"), "tensor"),
            P(("dp", "sub"), "tensor"),
            P(("dp", "sub"), "tensor"),
        ),
        out_specs=P(("groups", "dp", "sub"), "tensor"),
        check_vma=False,
    )
```

```python
import functools

import jax
import jax.numpy as jnp
from jax import lax
from jax.experimental import pallas as pl
from jax.experimental.pallas import tpu as pltpu
from jax.sharding import PartitionSpec as P

LANE_SHARES = (7, 5, 3, 1)
VMEM = 52 * 1024 * 1024
SMALL = 1_750_000
UP_SHARES = (7, 6)
CHEAP = pl.CostEstimate(flops=1, bytes_accessed=1, transcendentals=0)
ANY = pl.BlockSpec(memory_space=pl.ANY)
HBM = pl.BlockSpec(memory_space=pltpu.HBM)


def shifted(block, axis, distance):
    devices = range(lax.axis_size(axis))
    route = [((i - distance) % len(devices), i) for i in devices]
    return lax.ppermute(block, axis, route)


def across(block):
    return shifted(block, "groups", 1)


def tied(value, *earlier):
    return lax.optimization_barrier((value, *earlier))[0] if earlier else value


def cuts(total, unit, shares):
    units, whole, done, marks = total // unit, sum(shares), 0, [0]
    for share in shares:
        done += share
        marks.append(units * done // whole * unit)
    marks[-1] = total
    return list(zip(marks[:-1], marks[1:]))


def call(kernel, operands, outs, out_specs, scratch, aliases=None):
    aliases = aliases or {}
    return pl.pallas_call(
        kernel,
        in_specs=[pl.BlockSpec(memory_space=pltpu.SMEM)]
        + [
            ANY if i in aliases or array.size * array.dtype.itemsize < SMALL else HBM
            for i, array in enumerate(operands)
        ][1:],
        out_specs=out_specs,
        out_shape=outs,
        scratch_shapes=scratch,
        input_output_aliases=aliases,
        compiler_params=pltpu.CompilerParams(vmem_limit_bytes=VMEM),
        cost_estimate=CHEAP,
    )(*operands)


def pieces_kernel(cuts_of, side_ref, *refs):
    count = len(cuts_of)
    sources, outs, sems = refs[:-1 - count], refs[-1 - count : -1], refs[-1]
    side = side_ref[0]
    copies = []
    for i, (source, base, offset, lanes) in enumerate(cuts_of):
        start = pl.multiple_of(base + (side if offset > 0 else 1 - side) * abs(offset), 128)
        copies.append(
            pltpu.make_async_copy(
                sources[source].at[:, pl.ds(start, lanes)], outs[i], sems.at[i]
            )
        )
    for copy in copies:
        copy.start()
    for copy in copies:
        copy.wait()


def cut_pieces(side, arrays, cuts_of):
    return call(
        functools.partial(pieces_kernel, cuts_of),
        (side, *arrays),
        [
            jax.ShapeDtypeStruct((arrays[i].shape[0], lanes), arrays[i].dtype)
            for i, _, _, lanes in cuts_of
        ],
        [ANY] * len(cuts_of),
        [pltpu.SemaphoreType.DMA((len(cuts_of),))],
    )


def products_kernel(halved, outs, block, steps, side_ref, *refs):
    operands, out_refs, total = refs[: -1 - outs], refs[-1 - outs : -1], refs[-1]
    side = side_ref[0]
    total[...] = jnp.zeros_like(total)

    def body(*blocks):
        units = [ref[...] for ref in blocks[len(halved) :]]
        units = units[0] if len(units) == 1 else jnp.concatenate(units, axis=0)
        at = 0
        for ref in blocks[: len(halved)]:
            rows = ref.shape[0]
            total[at : at + rows] += lax.dot_general(
                ref[...], units, (((1,), (1,)), ((), ())), preferred_element_type=jnp.float32
            )
            at += rows

    pltpu.emit_pipeline(
        body,
        grid=(steps,),
        in_specs=[
            pl.BlockSpec(
                (ref.shape[0], block),
                (lambda k: (0, side * steps + k))
                if i < len(halved) and halved[i]
                else (lambda k: (0, k)),
            )
            for i, ref in enumerate(operands)
        ],
    )(*operands)
    at = 0
    for out_ref in out_refs:
        rows = out_ref.shape[0]
        out_ref[...] = total[at : at + rows].astype(out_ref.dtype)
        at += rows


def products(side, row_sets, halved, unit_sets, out_types):
    width = unit_sets[0].shape[1]
    block = 1024 if width % 1024 == 0 else width
    count = sum(u.shape[0] for u in unit_sets)
    rows = sum(r.shape[0] for r in row_sets)
    part = rows // len(out_types)
    return call(
        functools.partial(
            products_kernel, halved, len(out_types), block, width // block
        ),
        (side, *row_sets, *unit_sets),
        [jax.ShapeDtypeStruct((part, count), t) for t in out_types],
        [pl.BlockSpec(memory_space=pltpu.VMEM)] * len(out_types),
        [pltpu.VMEM((rows, count), jnp.float32)],
    )


def blocks_of(parts):
    found = []
    for i, (a, b) in enumerate(parts):
        half = (b - a) // 2
        size = 512 if half % 512 == 0 else 256 if half % 256 == 0 else 128
        for j in range(2):
            for at in range(0, half, size):
                found.append((i, j, at, size, a + j * half + at))
    return found


def output_kernel(parts, side_ref, *refs):
    hidden, down, arrived = refs[:2], refs[2], refs[3 : 3 + len(parts)]
    out, rows, near, far, result, sems, row_sems = refs[-7:]
    units = down.shape[0]
    share = units // 2
    core = side_ref[1]
    blocks = blocks_of(parts)
    row_copies = [
        pltpu.make_async_copy(hidden[i], rows.at[i], row_sems.at[i]) for i in range(2)
    ]
    loads, stores, spots, at = [], [], [], 0
    for n, (i, j, lane, size, column) in enumerate(blocks):
        spot = pl.ds(at, size)
        spots.append(slice(at, at + size))
        at += size
        loads.append(
            [
                pltpu.make_async_copy(
                    down.at[:, pl.ds(column, size)], near.at[:, spot], sems.at[0, n]
                )
            ]
            + [
                pltpu.make_async_copy(
                    arrived[i].at[
                        pl.ds(pl.multiple_of(j * units + from_core * share, 16), share),
                        pl.ds(lane, size),
                    ],
                    far.at[pl.ds(k * share, share), spot],
                    sems.at[1 + k, n],
                )
                for k, from_core in enumerate((core, 1 - core))
            ]
        )
        stores.append(
            pltpu.make_async_copy(
                result.at[:, spot], out.at[:, pl.ds(column, size)], sems.at[3, n]
            )
        )
    for copy in row_copies:
        copy.start()
    for group in loads:
        for copy in group:
            copy.start()
    for copy in row_copies:
        copy.wait()
    for n, spot in enumerate(spots):
        for copy in loads[n]:
            copy.wait()
        total = jnp.dot(rows[0], near[:, spot], preferred_element_type=jnp.float32)
        total += jnp.dot(rows[1], far[:, spot], preferred_element_type=jnp.float32)
        result[:, spot] = total.astype(result.dtype)
        stores[n].start()
    for copy in stores:
        copy.wait()


def output_part(result, parts, side, hidden, down, arrived):
    rows, units, width = hidden[0].shape[0], down.shape[0], down.shape[1]
    lanes = sum(b - a for a, b in parts)
    count = len(blocks_of(parts))
    operands = (side, *hidden, down, *arrived)
    aliases = None
    if result is not None:
        aliases = {len(operands): 0}
        operands += (result,)
    return call(
        functools.partial(output_kernel, parts),
        operands,
        jax.ShapeDtypeStruct((rows, width), jnp.bfloat16),
        ANY,
        [
            pltpu.VMEM((2, rows, units), jnp.bfloat16),
            pltpu.VMEM((units, lanes), jnp.bfloat16),
            pltpu.VMEM((units, lanes), jnp.bfloat16),
            pltpu.VMEM((rows, lanes), jnp.bfloat16),
            pltpu.SemaphoreType.DMA((4, count)),
            pltpu.SemaphoreType.DMA((2,)),
        ],
        aliases,
    )


def over_slices(partial_value):
    return [
        shifted(partial_value, "tensor", distance)
        for distance in range(1, lax.axis_size("tensor"))
    ]


def summed(partial_value, sent):
    total = partial_value.astype(jnp.float32)
    for block in sent:
        total = total + block.astype(jnp.float32)
    return total


def gated(gate, up):
    return (jax.nn.silu(gate) * up).astype(jnp.bfloat16)


def on_device(tokens, gate_weight, up_weight, down_weight):
    width, rows = gate_weight.shape[1], tokens.shape[0]
    half = width // 2
    units = gate_weight.shape[0]
    side = jnp.stack([lax.axis_index("groups"), lax.axis_index("sub")]).astype(jnp.int32)
    lane_cuts = tuple((2 * a, 2 * b) for a, b in cuts(half, 128, LANE_SHARES))

    (gate_piece,) = cut_pieces(side, (gate_weight,), ((0, 0, half, half),))
    up_piece, swapped = cut_pieces(
        side,
        (tied(up_weight, gate_piece), tokens),
        ((0, 0, half, half), (1, 0, -half, half)),
    )
    down_pieces = cut_pieces(
        side,
        (tied(down_weight, swapped),),
        tuple((0, a, (b - a) // 2, (b - a) // 2) for a, b in lane_cuts),
    )
    gate_next = shifted(gate_piece, "dp", 1)
    up_next = [shifted(up_piece[a:b], "dp", 1) for a, b in cuts(units, 16, UP_SHARES)]
    down_next = [shifted(piece, "dp", 1) for piece in down_pieces]

    def both_cores(block):
        return lax.all_gather(block, "sub", axis=0, tiled=True)

    def all_four(block):
        return lax.all_gather(block, ("groups", "sub"), axis=0, tiled=True)

    def mate(block, parts):
        return [
            shifted(block[a:b], "sub", 1)
            for a, b in cuts(block.shape[0], 16, (1,) * parts)
        ]

    gate_here, up_here, down_here = (
        both_cores(tied(w, gate_piece)) for w in (gate_weight, up_weight, down_weight)
    )
    tokens_other = [across(swapped[a:b]) for a, b in cuts(rows, 16, (1, 1))]

    def joint(unit_sets):
        return products(
            side,
            [tokens, *tokens_other],
            [True] + [False] * len(tokens_other),
            unit_sets,
            [jnp.float32, jnp.bfloat16],
        )

    def one_slice(kept, given):
        return (kept + given.astype(jnp.float32)).astype(jnp.bfloat16)

    gate_own = gate_next
    gate_mate = mate(gate_own, 4)
    (mine,) = products(
        side, [tied(tokens, gate_own)], [False], [gate_here, up_here], [jnp.bfloat16]
    )
    mine_sent = over_slices(mine)

    up_own = [tied(up_next[0], mine)]
    up_mate = mate(up_own[0], 2)
    tokens_other = [tied(block, up_own[0]) for block in tokens_other]
    gate_kept, gate_sent = joint([gate_own, *gate_mate])
    gate_given = across(gate_sent)
    pre = summed(mine, [tied(block, gate_sent) for block in mine_sent])
    count = pre.shape[1] // 2
    here = gated(pre[:, :count], pre[:, count:])

    up_own.append(tied(up_next[1], here))
    up_mate += mate(up_own[1], 2)
    gate_slice = one_slice(gate_kept, tied(gate_given, up_own[1]))
    gate_slices = over_slices(gate_slice)
    up_mate = [tied(block, gate_slice) for block in up_mate]
    up_kept, up_sent = joint([*up_own, *up_mate])
    up_given = across(up_sent)

    gathered = []
    gate_slices = [tied(block, up_sent) for block in gate_slices]
    up_slice = one_slice(up_kept, tied(up_given, *gate_slices))
    now = tied(down_next[0], up_slice)
    gathered.append(all_four(now))
    up_slices = over_slices(up_slice)
    there = gated(summed(gate_slice, gate_slices), summed(up_slice, up_slices))
    now = tied(down_next[1], there)
    gathered.append(all_four(now))
    now = tied(down_next[2], now)
    gathered.append(all_four(now))

    hidden = (here, there)
    result = output_part(
        None, lane_cuts[:1], side, hidden, down_here, [tied(gathered[0], now)]
    )
    now = tied(down_next[3], result)
    gathered.append(all_four(now))
    result = output_part(
        result, lane_cuts[1:2], side, hidden, down_here, [tied(gathered[1], now)]
    )
    return output_part(result, lane_cuts[2:], side, hidden, down_here, gathered[2:])


def solution(mesh):
    return jax.shard_map(
        on_device,
        mesh=mesh,
        in_specs=(
            P(("groups", "dp", "sub"), "tensor"),
            P(("dp", "sub"), "tensor"),
            P(("dp", "sub"), "tensor"),
            P(("dp", "sub"), "tensor"),
        ),
        out_specs=P(("groups", "dp", "sub"), "tensor"),
        check_vma=False,
    )
```

```python
import functools

import jax
import jax.numpy as jnp
from jax import lax
from jax.experimental import pallas as pl
from jax.experimental.pallas import tpu as pltpu
from jax.sharding import PartitionSpec as P

ROW_SHARES = (1, 2, 2, 2, 2, 2, 2)
LANE_SHARES = (4, 4, 3, 3, 2)
QUEUE = 2
SLOTS = 3
VMEM = 52 * 1024 * 1024
ANY = pl.BlockSpec(memory_space=pl.ANY)


def shifted(block, axis, distance):
    devices = range(lax.axis_size(axis))
    route = [((i - distance) % len(devices), i) for i in devices]
    return lax.ppermute(block, axis, route)


def mate(block):
    return shifted(block, "sub", 1)


def across(block):
    return shifted(block, "groups", 1)


def tied(value, *earlier):
    return lax.optimization_barrier((value, *earlier))[0] if earlier else value


def cuts(total, unit, shares):
    units, whole, done, marks = total // unit, sum(shares), 0, [0]
    for share in shares:
        done += share
        marks.append(units * done // whole * unit)
    marks[-1] = total
    return list(zip(marks[:-1], marks[1:]))


def call(kernel, operands, in_specs, out, out_spec, scratch, aliases):
    return pl.pallas_call(
        kernel,
        in_specs=in_specs,
        out_specs=out_spec,
        out_shape=out,
        scratch_shapes=scratch,
        input_output_aliases=aliases,
        compiler_params=pltpu.CompilerParams(vmem_limit_bytes=VMEM),
        cost_estimate=pl.CostEstimate(flops=1, bytes_accessed=1, transcendentals=0),
    )(*operands)


def products_kernel(sets, block, *refs):
    operands, (out, rows, units, total, sems) = refs[:-5], refs[-5:]
    steps = operands[0].shape[1] // block

    def loads(step):
        slot, found, at = step % SLOTS, [], [0, 0]
        for i, ref in enumerate(operands):
            kind = 0 if i < sets else 1
            spot = pl.ds(at[kind], ref.shape[0])
            found.append(
                pltpu.make_async_copy(
                    ref.at[:, pl.ds(step * block, block)],
                    (rows, units)[kind].at[slot, spot],
                    sems.at[slot, i],
                )
            )
            at[kind] += ref.shape[0]
        return found

    for step in range(min(SLOTS - 1, steps)):
        for copy in loads(step):
            copy.start()
    for step in range(steps):
        if step + SLOTS - 1 < steps:
            for copy in loads(step + SLOTS - 1):
                copy.start()
        for copy in loads(step):
            copy.wait()
        value = lax.dot_general(
            rows[step % SLOTS],
            units[step % SLOTS],
            (((1,), (1,)), ((), ())),
            preferred_element_type=jnp.float32,
        )
        if step > 0:
            value += total[...]
        if step < steps - 1:
            total[...] = value
        else:
            out[...] = value.astype(out.dtype)


def products(row_sets, unit_sets):
    width = row_sets[0].shape[1]
    block = 1024 if width % 1024 == 0 else width
    shape = (sum(r.shape[0] for r in row_sets), sum(u.shape[0] for u in unit_sets))
    operands = (*row_sets, *unit_sets)
    return call(
        functools.partial(products_kernel, len(row_sets), block),
        operands,
        [ANY] * len(operands),
        jax.ShapeDtypeStruct(shape, jnp.bfloat16),
        pl.BlockSpec(memory_space=pltpu.VMEM),
        [
            pltpu.VMEM((SLOTS, shape[0], block), jnp.bfloat16),
            pltpu.VMEM((SLOTS, shape[1], block), jnp.bfloat16),
            pltpu.VMEM(shape, jnp.float32),
            pltpu.SemaphoreType.DMA((SLOTS, len(operands))),
        ],
        {},
    )


def blocks_of(parts):
    found = []
    for i, (a, b, whole) in enumerate(parts):
        half = (b - a) // 2
        size = 512 if half % 512 == 0 else 256 if half % 256 == 0 else 128
        for k in range(2):
            for lane in range(0, half, size):
                if whole:
                    found.append((i, 0, k * half + lane, size, (a + k * half + lane, 0)))
                else:
                    found.append((i, k, lane, size, (a + k * half + lane, half - 2 * k * half)))
    return found


def output_kernel(parts, side_ref, *refs):
    hidden, down = refs[:4], refs[4:6]
    arrived = refs[6 : 6 + 4 * len(parts)]
    out, weights, result, sems = refs[-4:]
    share = down[0].shape[0]
    side = side_ref[0]
    loads, stores, spots, at = [], [], [], 0
    for n, (i, k, lane, size, (fixed, turn)) in enumerate(blocks_of(parts)):
        column = pl.ds(pl.multiple_of(fixed + side * turn, 128), size)
        spot = pl.ds(at, size)
        spots.append(slice(at, at + size))
        at += size
        sources = [ref.at[:, column] for ref in down]
        sources += [arrived[4 * i + 2 * m + k].at[:, pl.ds(lane, size)] for m in range(2)]
        loads.append(
            [
                pltpu.make_async_copy(source, weights.at[m, :, spot], sems.at[m, n])
                for m, source in enumerate(sources)
            ]
        )
        stores.append(
            pltpu.make_async_copy(result.at[:, spot], out.at[:, column], sems.at[4, n])
        )
    for group in loads:
        for copy in group:
            copy.start()
    for n, spot in enumerate(spots):
        for copy in loads[n]:
            copy.wait()
        total = None
        for m in range(4):
            term = jnp.dot(
                hidden[m][...], weights[m, :, spot], preferred_element_type=jnp.float32
            )
            total = term if total is None else total + term
        result[:, spot] = total.astype(result.dtype)
        stores[n].start()
    for copy in stores:
        copy.wait()


def output_part(result, parts, side, hidden, down, arrived):
    rows, units, width = hidden[0].shape[0], down[0].shape[0], down[0].shape[1]
    lanes = sum(b - a for a, b, _ in parts)
    operands = [side, *hidden, *down, *arrived]
    in_specs = (
        [pl.BlockSpec(memory_space=pltpu.SMEM)]
        + [pl.BlockSpec(memory_space=pltpu.VMEM)] * 4
        + [ANY] * (2 + len(arrived))
    )
    aliases = {}
    if result is not None:
        aliases = {len(operands): 0}
        operands.append(result)
        in_specs.append(ANY)
    return call(
        functools.partial(output_kernel, parts),
        operands,
        in_specs,
        jax.ShapeDtypeStruct((rows, width), jnp.bfloat16),
        ANY,
        [
            pltpu.VMEM((4, units, lanes), jnp.bfloat16),
            pltpu.VMEM((rows, lanes), jnp.bfloat16),
            pltpu.SemaphoreType.DMA((5, len(blocks_of(parts)))),
        ],
        aliases,
    )


def over_slices(partial_value):
    return [
        shifted(partial_value, "tensor", distance)
        for distance in range(1, lax.axis_size("tensor"))
    ]


def summed(partial_value, sent):
    total = partial_value.astype(jnp.float32)
    for block in sent:
        total = total + block.astype(jnp.float32)
    return total


def gated(gate, up):
    return (jax.nn.silu(gate) * up).astype(jnp.bfloat16)


def on_device(tokens, gate_weight, up_weight, down_weight):
    units, width = gate_weight.shape
    rows = tokens.shape[0]
    group = lax.axis_index("groups").astype(jnp.int32)
    first = group == 0
    side = group.reshape(1)

    row_cuts = cuts(units, 16, ROW_SHARES)
    lane_cuts = [(2 * a, 2 * b) for a, b in cuts(width // 2, 128, LANE_SHARES)]
    count = len(row_cuts)
    total_count = count + len(lane_cuts)
    last = total_count - 1

    def piece(i, *after):
        if i < count:
            a, b = row_cuts[i]
            gate, up = gate_weight, up_weight
            if after:
                gate, up = lax.optimization_barrier((gate, up, *after))[:2]
            return jnp.where(first, gate[a:b], up[a:b])
        a, b = lane_cuts[i - count]
        mid = (a + b) // 2
        down = tied(down_weight, *after)
        if i == last:
            return down[:, a:b]
        return jnp.where(first, down[:, a:mid], down[:, mid:b])

    pieces = [piece(0)]
    pieces.append(piece(1, pieces[0]))
    pieces += [piece(i, pieces[1]) for i in range(2, total_count)]
    waiting = [shifted(pieces[i], "dp", 1) for i in range(QUEUE)]
    landed, crossed, mates, crossed_mates = [], {}, {}, {}

    def advance(*after):
        i = len(landed)
        held = [*after, *landed[-1:]]
        for swapped, j in ((crossed, i - 2), (mates, i - 2), (crossed_mates, i - 4)):
            if j in swapped:
                held.append(swapped[j])
        block = tied(waiting[i], *held)
        landed.append(block)
        if i < last:
            crossed[i] = across(block)
        if i >= count:
            mates[i] = mate(block)
        if i - 2 in range(count, last):
            crossed_mates[i - 2] = mate(tied(crossed[i - 2], block))
        if i + QUEUE < total_count:
            waiting.append(shifted(tied(pieces[i + QUEUE], block), "dp", 1))
        return block

    def local(partial_value, sent):
        pre = summed(partial_value, sent)
        return gated(pre[:, :units], pre[:, units:])

    def batch(lo, hi, now):
        held = [landed[i] for i in range(lo, hi)] + [crossed[i] for i in range(lo, hi)]
        held = lax.optimization_barrier((*held, now))[:-1]
        value = products([tokens, tokens_mate], held)
        return value, over_slices(value)

    def activated(partial_value, sent):
        pre = summed(partial_value, sent)
        half = pre.shape[1] // 2
        left, right = pre[:, :half], pre[:, half:]
        return gated(jnp.where(first, left, right), jnp.where(first, right, left))

    tokens_mate = mate(tied(tokens, pieces[0]))
    down_mate = mate(tied(down_weight, pieces[1]))
    now = advance()
    mine = products([tied(tokens, now)], [gate_weight, up_weight])
    mine_sent = over_slices(mine)
    now = advance(mine)
    theirs = products([tied(tokens_mate, now)], [gate_weight, up_weight])
    theirs_sent = over_slices(theirs)
    now = advance(theirs)
    here = local(mine, [tied(block, now) for block in mine_sent])
    now = advance(here)
    here_mate = mate(local(theirs, [tied(block, now) for block in theirs_sent]))
    now = advance()
    now = advance(here_mate)
    early, early_sent = batch(0, 4, now)
    now = advance(early)
    there = [activated(early, [tied(block, now) for block in early_sent])]
    now = advance(there[0], down_mate)
    late, late_sent = batch(4, count, now)
    now = advance(late)
    now = advance()
    there.append(activated(late, [tied(block, now) for block in late_sent]))
    there = jnp.concatenate(there, axis=1)
    there_mate = mate(there[rows:])
    there = there[:rows]
    now = advance(there)
    there_mate = tied(there_mate, now)

    def write(result, *which):
        parts, arrived = [], []
        for n in which:
            i = count + n
            parts.append((*lane_cuts[n], i == last))
            if i == last:
                arrived += [landed[i], landed[i], mates[i], mates[i]]
            else:
                if i not in crossed_mates:
                    crossed_mates[i] = mate(crossed[i])
                arrived += [landed[i], crossed[i], mates[i], crossed_mates[i]]
        return output_part(
            result,
            tuple(parts),
            side,
            [here, here_mate, there, there_mate],
            [down_weight, down_mate],
            arrived,
        )

    result = write(None, 0)
    now = advance(result)
    result = write(result, 1)
    crossed[last - 1] = tied(crossed[last - 1], crossed_mates[last - 2])
    result = write(result, 2, 4)
    return write(result, 3)


def solution(mesh):
    return jax.shard_map(
        on_device,
        mesh=mesh,
        in_specs=(
            P(("groups", "dp", "sub"), "tensor"),
            P(("dp", "sub"), "tensor"),
            P(("dp", "sub"), "tensor"),
            P(("dp", "sub"), "tensor"),
        ),
        out_specs=P(("groups", "dp", "sub"), "tensor"),
        check_vma=False,
    )
```

```python
import functools

import jax
import jax.numpy as jnp
from jax import lax
from jax.experimental import pallas as pl
from jax.experimental.pallas import tpu as pltpu
from jax.sharding import PartitionSpec as P

ROW_SHARES = (2, 2, 2, 2, 2, 2, 1)
LANE_SHARES = (5, 5, 3, 3)
QUEUE = 3
SLOTS = 3
VMEM = 52 * 1024 * 1024
ANY = pl.BlockSpec(memory_space=pl.ANY)


def shifted(block, axis, distance):
    devices = range(lax.axis_size(axis))
    route = [((i - distance) % len(devices), i) for i in devices]
    return lax.ppermute(block, axis, route)


def mate(block):
    return shifted(block, "sub", 1)


def across(block):
    return shifted(block, "groups", 1)


def tied(value, *earlier):
    return lax.optimization_barrier((value, *earlier))[0] if earlier else value


def cuts(total, unit, shares):
    units, whole, done, marks = total // unit, sum(shares), 0, [0]
    for share in shares:
        done += share
        marks.append(units * done // whole * unit)
    marks[-1] = total
    return list(zip(marks[:-1], marks[1:]))


def call(kernel, operands, in_specs, out, out_spec, scratch, aliases):
    return pl.pallas_call(
        kernel,
        in_specs=in_specs,
        out_specs=out_spec,
        out_shape=out,
        scratch_shapes=scratch,
        input_output_aliases=aliases,
        compiler_params=pltpu.CompilerParams(vmem_limit_bytes=VMEM),
        cost_estimate=pl.CostEstimate(flops=1, bytes_accessed=1, transcendentals=0),
    )(*operands)


def products_kernel(sets, block, *refs):
    operands, (out, rows, units, total, sems) = refs[:-5], refs[-5:]
    steps = operands[0].shape[1] // block

    def loads(step):
        slot, found, at = step % SLOTS, [], [0, 0]
        for i, ref in enumerate(operands):
            kind = 0 if i < sets else 1
            spot = pl.ds(at[kind], ref.shape[0])
            found.append(
                pltpu.make_async_copy(
                    ref.at[:, pl.ds(step * block, block)],
                    (rows, units)[kind].at[slot, spot],
                    sems.at[slot, i],
                )
            )
            at[kind] += ref.shape[0]
        return found

    for step in range(min(SLOTS - 1, steps)):
        for copy in loads(step):
            copy.start()
    for step in range(steps):
        if step + SLOTS - 1 < steps:
            for copy in loads(step + SLOTS - 1):
                copy.start()
        for copy in loads(step):
            copy.wait()
        value = lax.dot_general(
            rows[step % SLOTS],
            units[step % SLOTS],
            (((1,), (1,)), ((), ())),
            preferred_element_type=jnp.float32,
        )
        if step > 0:
            value += total[...]
        if step < steps - 1:
            total[...] = value
        else:
            out[...] = value.astype(out.dtype)


def products(row_sets, unit_sets):
    width = row_sets[0].shape[1]
    block = 1024 if width % 1024 == 0 else width
    shape = (sum(r.shape[0] for r in row_sets), sum(u.shape[0] for u in unit_sets))
    operands = (*row_sets, *unit_sets)
    return call(
        functools.partial(products_kernel, len(row_sets), block),
        operands,
        [ANY] * len(operands),
        jax.ShapeDtypeStruct(shape, jnp.bfloat16),
        pl.BlockSpec(memory_space=pltpu.VMEM),
        [
            pltpu.VMEM((SLOTS, shape[0], block), jnp.bfloat16),
            pltpu.VMEM((SLOTS, shape[1], block), jnp.bfloat16),
            pltpu.VMEM(shape, jnp.float32),
            pltpu.SemaphoreType.DMA((SLOTS, len(operands))),
        ],
        {},
    )


def blocks_of(parts):
    found = []
    for i, (a, half, own, other) in enumerate(parts):
        arrays = [(0, lanes) for lanes in own] + [(1, lanes) for lanes in other]
        filled = [0, 0]
        for n, (k, lanes) in enumerate(arrays):
            for lane in range(0, lanes, 512):
                size = min(512, lanes - lane)
                turn = half - 2 * k * half if other else 0
                found.append((i, n, lane, size, (a + k * half + filled[k] + lane, turn)))
            filled[k] += lanes
    return found


def output_kernel(parts, side_ref, *refs):
    hidden, down = refs[:4], refs[4:6]
    arrived, at = [], 6
    for _, _, own, other in parts:
        count = len(own) + len(other)
        arrived.append((refs[at : at + count], refs[at + count : at + 2 * count]))
        at += 2 * count
    out, weights, result, sems = refs[-4:]
    share = down[0].shape[0]
    side = side_ref[0]
    loads, stores, spots, at = [], [], [], 0
    for n, (i, array, lane, size, (fixed, turn)) in enumerate(blocks_of(parts)):
        column = pl.ds(pl.multiple_of(fixed + side * turn, 128), size)
        spot = pl.ds(at, size)
        spots.append(slice(at, at + size))
        at += size
        sources = [ref.at[:, column] for ref in down]
        sources += [arrays[array].at[:, pl.ds(lane, size)] for arrays in arrived[i]]
        loads.append(
            [
                pltpu.make_async_copy(source, weights.at[m, :, spot], sems.at[m, n])
                for m, source in enumerate(sources)
            ]
        )
        stores.append(
            pltpu.make_async_copy(result.at[:, spot], out.at[:, column], sems.at[4, n])
        )
    for group in loads:
        for copy in group:
            copy.start()
    for n, spot in enumerate(spots):
        for copy in loads[n]:
            copy.wait()
        total = None
        for m in range(4):
            term = jnp.dot(
                hidden[m][...], weights[m, :, spot], preferred_element_type=jnp.float32
            )
            total = term if total is None else total + term
        result[:, spot] = total.astype(result.dtype)
        stores[n].start()
    for copy in stores:
        copy.wait()


def output_part(result, parts, side, hidden, down, arrived):
    rows, units, width = hidden[0].shape[0], down[0].shape[0], down[0].shape[1]
    lanes = sum(sum(own) + sum(other) for _, _, own, other in parts)
    operands = [side, *hidden, *down, *arrived]
    in_specs = (
        [pl.BlockSpec(memory_space=pltpu.SMEM)]
        + [pl.BlockSpec(memory_space=pltpu.VMEM)] * 4
        + [ANY] * (2 + len(arrived))
    )
    aliases = {}
    if result is not None:
        aliases = {len(operands): 0}
        operands.append(result)
        in_specs.append(ANY)
    return call(
        functools.partial(output_kernel, parts),
        operands,
        in_specs,
        jax.ShapeDtypeStruct((rows, width), jnp.bfloat16),
        ANY,
        [
            pltpu.VMEM((4, units, lanes), jnp.bfloat16),
            pltpu.VMEM((rows, lanes), jnp.bfloat16),
            pltpu.SemaphoreType.DMA((5, len(blocks_of(parts)))),
        ],
        aliases,
    )


def over_slices(partial_value):
    return [
        shifted(partial_value, "tensor", distance)
        for distance in range(1, lax.axis_size("tensor"))
    ]


def summed(partial_value, sent):
    total = partial_value.astype(jnp.float32)
    for block in sent:
        total = total + block.astype(jnp.float32)
    return total


def gated(gate, up):
    return (jax.nn.silu(gate) * up).astype(jnp.bfloat16)


def on_device(tokens, gate_weight, up_weight, down_weight):
    units, width = gate_weight.shape
    rows = tokens.shape[0]
    group = lax.axis_index("groups").astype(jnp.int32)
    first = group == 0
    side = group.reshape(1)

    row_cuts = cuts(units, 16, ROW_SHARES)
    lane_cuts = [(2 * a, 2 * b) for a, b in cuts(width // 2, 128, LANE_SHARES)]
    count = len(row_cuts)
    total_count = count + len(lane_cuts)
    last = total_count - 1

    def piece(i, *after):
        if i < count:
            a, b = row_cuts[i]
            gate, up = gate_weight, up_weight
            if after:
                gate, up = lax.optimization_barrier((gate, up, *after))[:2]
            return jnp.where(first, gate[a:b], up[a:b])
        a, b = lane_cuts[i - count]
        mid = (a + b) // 2
        down = tied(down_weight, *after)
        if i == last:
            return down[:, a:b]
        return jnp.where(first, down[:, a:mid], down[:, mid:b])

    pieces = [piece(0)]
    pieces.append(piece(1, pieces[0]))
    pieces += [piece(i, pieces[1]) for i in range(2, total_count)]
    waiting = [shifted(pieces[i], "dp", 1) for i in range(QUEUE)]
    landed, crossed, mates, crossed_mates = [], {}, {}, {}

    def in_two(block):
        mid = max(128, block.shape[1] // 256 * 128)
        if mid >= block.shape[1]:
            return [block]
        return [block[:, :mid], block[:, mid:]]

    def advance(*after):
        i = len(landed)
        held = [*after, *landed[-1:]]
        if 0 <= i - QUEUE < count:
            held.append(crossed[i - QUEUE])
        block = tied(waiting[i], *held)
        landed.append(block)
        if i < last:
            crossed[i] = across(block)
        if i >= count:
            mates[i] = mate(block)
        if i + QUEUE < total_count:
            waiting.append(shifted(tied(pieces[i + QUEUE], block), "dp", 1))
        return block

    def pass_on(n, *after):
        i = count + n
        crossed[i] = tied(crossed[i], *after)
        crossed_mates[i] = [mate(part) for part in in_two(crossed[i])]
        return crossed[i]

    def local(partial_value, sent):
        pre = summed(partial_value, sent)
        return gated(pre[:, :units], pre[:, units:])

    def batch(lo, hi, now):
        held = [landed[i] for i in range(lo, hi)]
        held += [crossed[i] for i in range(lo, hi)]
        held = lax.optimization_barrier((*held, now))[:-1]
        value = products([tokens, tokens_mate], held)
        return value, over_slices(value)

    def activated(partial_value, sent):
        pre = summed(partial_value, sent)
        half = pre.shape[1] // 2
        left, right = pre[:, :half], pre[:, half:]
        return gated(jnp.where(first, left, right), jnp.where(first, right, left))

    tokens_mate = mate(tied(tokens, pieces[0]))
    down_mate = mate(tied(down_weight, pieces[1]))
    mine = products([tokens], [gate_weight, up_weight])
    mine_sent = over_slices(mine)
    advance(mine)
    now = advance()
    theirs = products([tied(tokens_mate, now)], [gate_weight, up_weight])
    theirs_sent = over_slices(theirs)
    advance(theirs)
    now = advance()
    here = local(mine, [tied(block, now) for block in mine_sent])
    now = advance(here)
    early, early_sent = batch(0, 3, now)
    now = advance(early)
    here_mate = mate(local(theirs, [tied(block, now) for block in theirs_sent]))
    now = advance()
    there = [activated(early, [tied(block, now) for block in early_sent])]
    now = advance(there[0], here_mate)
    late, late_sent = batch(3, count, now)
    now = advance(late, down_mate)
    now = pass_on(0, now)
    now = advance(now)
    there.append(activated(late, [tied(block, now) for block in late_sent]))
    there = jnp.concatenate(there, axis=1)
    there_mate = mate(there[rows:])
    there = there[:rows]

    def write(result, *which):
        parts, arrived = [], []
        for n in which:
            i = count + n
            a, b = lane_cuts[n]
            if i == last:
                parts.append((a, (b - a) // 2, (b - a,), ()))
                arrived += [landed[i], mates[i]]
            else:
                half = (b - a) // 2
                lanes = tuple(part.shape[1] for part in crossed_mates[i])
                parts.append((a, half, (half,), lanes))
                arrived += [landed[i], *in_two(crossed[i]), mates[i], *crossed_mates[i]]
        return output_part(
            result,
            tuple(parts),
            side,
            [here, here_mate, there, there_mate],
            [down_weight, down_mate],
            arrived,
        )

    result = write(None, 0)
    pass_on(1, result)
    result = write(result, 1)
    now = advance(result)
    pass_on(2, now)
    return write(result, 2, 3)


def solution(mesh):
    return jax.shard_map(
        on_device,
        mesh=mesh,
        in_specs=(
            P(("groups", "dp", "sub"), "tensor"),
            P(("dp", "sub"), "tensor"),
            P(("dp", "sub"), "tensor"),
            P(("dp", "sub"), "tensor"),
        ),
        out_specs=P(("groups", "dp", "sub"), "tensor"),
        check_vma=False,
    )
```

```python
import functools

import jax
import jax.numpy as jnp
from jax import lax
from jax.experimental import pallas as pl
from jax.experimental.pallas import tpu as pltpu
from jax.sharding import PartitionSpec as P

FEATURE_SHARES = (11, 11, 11, 11, 10, 10)
LANE_SHARES = (10, 10, 6, 6)
QUEUE = 2
VMEM = 16 * 1024 * 1024
ANY = pl.BlockSpec(memory_space=pl.ANY)


def shifted(block, axis, distance):
    devices = range(lax.axis_size(axis))
    route = [((i - distance) % len(devices), i) for i in devices]
    return lax.ppermute(block, axis, route)


def mate(block):
    return shifted(block, "sub", 1)


def across(block):
    return shifted(block, "groups", 1)


def tied(value, *earlier):
    return lax.optimization_barrier((value, *earlier))[0] if earlier else value


def cuts(total, unit, shares):
    units, whole, done, marks = total // unit, sum(shares), 0, [0]
    for share in shares:
        done += share
        marks.append(units * done // whole * unit)
    marks[-1] = total
    return list(zip(marks[:-1], marks[1:]))


def call(kernel, operands, in_specs, out, out_spec, scratch, aliases):
    return pl.pallas_call(
        kernel,
        in_specs=in_specs,
        out_specs=out_spec,
        out_shape=out,
        scratch_shapes=scratch,
        input_output_aliases=aliases,
        compiler_params=pltpu.CompilerParams(vmem_limit_bytes=VMEM),
        cost_estimate=pl.CostEstimate(flops=1, bytes_accessed=1, transcendentals=0),
    )(*operands)


def products_kernel(sets, groups, spans, before, *refs):
    row_refs, unit_refs, total = refs[:sets], refs[sets : sets + groups * len(spans)], refs[-1]
    out = refs[-2]
    for step, (a, b) in enumerate(spans):
        units = jnp.concatenate(
            [ref[:, : b - a] for ref in unit_refs[step * groups : (step + 1) * groups]], axis=0
        )
        at = 0
        for ref in row_refs:
            spot = slice(at, at + ref.shape[0])
            at += ref.shape[0]
            value = lax.dot_general(
                ref[:, a:b], units, (((1,), (1,)), ((), ())), preferred_element_type=jnp.float32
            )
            if step > 0:
                value += total[spot]
            elif before:
                value += refs[-3][spot]
            if step < len(spans) - 1:
                total[spot] = value
            else:
                out[spot] = value.astype(out.dtype)


def products(row_sets, unit_sets, spans, before=None, out_type=jnp.bfloat16):
    groups = len(unit_sets) // len(spans)
    shape = (
        sum(r.shape[0] for r in row_sets),
        sum(u.shape[0] for u in unit_sets[:groups]),
    )
    operands = (*row_sets, *unit_sets)
    if before is not None:
        operands += (before,)
    whole = pl.BlockSpec(memory_space=pltpu.VMEM)
    return call(
        functools.partial(
            products_kernel, len(row_sets), groups, tuple(spans), before is not None
        ),
        operands,
        [whole] * len(operands),
        jax.ShapeDtypeStruct(shape, out_type),
        whole,
        [pltpu.VMEM(shape, jnp.float32)],
        {},
    )


def blocks_of(parts):
    found = []
    for i, (a, half, own, other) in enumerate(parts):
        arrays = [(0, lanes) for lanes in own] + [(1, lanes) for lanes in other]
        filled = [0, 0]
        for n, (k, lanes) in enumerate(arrays):
            for lane in range(0, lanes, 512):
                size = min(512, lanes - lane)
                turn = half - 2 * k * half if other else 0
                found.append((i, n, lane, size, (a + k * half + filled[k] + lane, turn)))
            filled[k] += lanes
    return found


def output_kernel(parts, side_ref, *refs):
    hidden, down = refs[:4], refs[4]
    arrived, at = [], 5
    for _, _, own, other in parts:
        count = len(own) + len(other)
        arrived.append((refs[at : at + count], refs[at + count : at + 2 * count]))
        at += 2 * count
    out, result, sems = refs[-3:]
    side, core = side_ref[0], side_ref[1]
    share = down.shape[0] // 2
    shares = [pl.ds(pl.multiple_of(c * share, 16), share) for c in (core, 1 - core)]
    stores, at = [], 0
    for n, (i, array, lane, size, (fixed, turn)) in enumerate(blocks_of(parts)):
        column = pl.ds(pl.multiple_of(fixed + side * turn, 128), size)
        spot = pl.ds(at, size)
        at += size
        total = None
        for m in range(4):
            if m < 2:
                weight = down[shares[m], column]
            else:
                weight = arrived[i][m - 2][array][:, lane : lane + size]
            term = jnp.dot(hidden[m][...], weight, preferred_element_type=jnp.float32)
            total = term if total is None else total + term
        result[:, spot] = total.astype(result.dtype)
        stores.append(
            pltpu.make_async_copy(result.at[:, spot], out.at[:, column], sems.at[n])
        )
        stores[-1].start()
    for copy in stores:
        copy.wait()


def output_part(result, parts, side, hidden, down, arrived):
    rows, width = hidden[0].shape[0], down.shape[1]
    lanes = sum(sum(own) + sum(other) for _, _, own, other in parts)
    operands = [side, *hidden, down, *arrived]
    in_specs = (
        [pl.BlockSpec(memory_space=pltpu.SMEM)]
        + [pl.BlockSpec(memory_space=pltpu.VMEM)] * (5 + len(arrived))
    )
    aliases = {}
    if result is not None:
        aliases = {len(operands): 0}
        operands.append(result)
        in_specs.append(ANY)
    return call(
        functools.partial(output_kernel, parts),
        operands,
        in_specs,
        jax.ShapeDtypeStruct((rows, width), jnp.bfloat16),
        ANY,
        [
            pltpu.VMEM((rows, lanes), jnp.bfloat16),
            pltpu.SemaphoreType.DMA((len(blocks_of(parts)),)),
        ],
        aliases,
    )


def over_slices(partial_value):
    return [
        shifted(partial_value, "tensor", distance)
        for distance in range(1, lax.axis_size("tensor"))
    ]


def summed(partial_value, sent):
    total = partial_value.astype(jnp.float32)
    for block in sent:
        total = total + block.astype(jnp.float32)
    return total


def gated(gate, up):
    return (jax.nn.silu(gate) * up).astype(jnp.bfloat16)


def on_device(tokens, gate_weight, up_weight, down_weight):
    units, width = gate_weight.shape
    rows = tokens.shape[0]
    group = lax.axis_index("groups").astype(jnp.int32)
    first = group == 0
    side = jnp.stack([group, lax.axis_index("sub").astype(jnp.int32)])

    spans = cuts(width, 128, FEATURE_SHARES)
    lane_cuts = [(2 * a, 2 * b) for a, b in cuts(width // 2, 128, LANE_SHARES)]
    count = len(spans)
    total_count = count + len(lane_cuts)
    last = total_count - 1

    def piece(i, *after):
        if i < count:
            a, b = spans[i]
            gate, up = gate_weight, up_weight
            if after:
                gate, up = lax.optimization_barrier((gate, up, *after))[:2]
            return jnp.where(first, gate[:, a:b], up[:, a:b])
        a, b = lane_cuts[i - count]
        mid = (a + b) // 2
        down = tied(down_weight, *after)
        if i == last:
            return down[:, a:b]
        return jnp.where(first, down[:, a:mid], down[:, mid:b])

    pieces = [piece(0)]
    pieces.append(piece(1, pieces[0]))
    pieces += [piece(i, pieces[1]) for i in range(2, total_count)]
    waiting = [shifted(pieces[i], "dp", 1) for i in range(QUEUE)]
    landed, crossed, mates, crossed_mates = [], {}, {}, {}

    def advance(*after):
        i = len(landed)
        held = [*after, *landed[-1:]]
        held += [crossed[j] for j in range(count) if j + 2 == i]
        block = tied(waiting[i], *held)
        landed.append(block)
        if i < last:
            crossed[i] = across(block)
        if i >= count:
            mates[i] = mate(block)
        if i + QUEUE < total_count:
            waiting.append(shifted(tied(pieces[i + QUEUE], block), "dp", 1))
        return block

    def pass_on(n, *after):
        i = count + n
        crossed[i] = tied(crossed[i], *after)
        crossed_mates[i] = mate(crossed[i])
        return crossed[i]

    def local(partial_value, sent):
        pre = summed(partial_value, sent)
        return gated(pre[:, :units], pre[:, units:])

    def batch(lo, hi, now, before=None, out_type=jnp.float32):
        held = [block for i in range(lo, hi) for block in (landed[i], crossed[i])]
        held = lax.optimization_barrier((*held, now))[:-1]
        return products([tokens, tokens_mate], held, spans[lo:hi], before, out_type)

    def activated(partial_value, sent):
        pre = summed(partial_value, sent)
        half = pre.shape[1] // 2
        left, right = pre[:, :half], pre[:, half:]
        return gated(jnp.where(first, left, right), jnp.where(first, right, left))

    tokens_mate = mate(tied(tokens, pieces[0]))
    down_here = lax.all_gather(tied(down_weight, pieces[1]), "sub", axis=0, tiled=True)

    def own_span(rows):
        return products([rows], [gate_weight, up_weight], [(0, width)])

    mine = own_span(tokens)
    now = advance(mine, *pieces[2:])
    theirs = own_span(tied(tokens_mate, now))
    value = jnp.concatenate([mine, theirs], axis=0)
    now = advance(value)
    sent = over_slices(value)
    now = advance()
    now = advance()
    here = local(value, [tied(block, now) for block in sent])
    here_mate = mate(here[rows:])
    here = here[:rows]
    value = batch(0, 2, now)
    now = advance(value, here)
    now = advance(here_mate)
    value = batch(2, 4, now, value)
    now = advance(value)
    value = batch(4, count, now, value, jnp.bfloat16)
    halves = [value[:rows], value[rows:]]
    sent = [over_slices(half) for half in halves]
    now = advance(value)
    now = pass_on(0, now)
    now = advance(now)
    there, given = (
        activated(half, [tied(block, now) for block in blocks])
        for half, blocks in zip(halves, sent)
    )
    there_mate = mate(given)

    def write(result, *which):
        parts, arrived = [], []
        for n in which:
            i = count + n
            a, b = lane_cuts[n]
            if i == last:
                parts.append((a, (b - a) // 2, (b - a,), ()))
                arrived += [landed[i], mates[i]]
            else:
                half = (b - a) // 2
                parts.append((a, half, (half,), (half,)))
                arrived += [landed[i], crossed[i], mates[i], crossed_mates[i]]
        return output_part(
            result,
            tuple(parts),
            side,
            [here, here_mate, there, there_mate],
            down_here,
            arrived,
        )

    result = write(None, 0)
    pass_on(1, result)
    result = write(result, 1)
    now = advance(result)
    result = write(result, 3)
    pass_on(2, now)
    return write(result, 2)


def solution(mesh):
    return jax.shard_map(
        on_device,
        mesh=mesh,
        in_specs=(
            P(("groups", "dp", "sub"), "tensor"),
            P(("dp", "sub"), "tensor"),
            P(("dp", "sub"), "tensor"),
            P(("dp", "sub"), "tensor"),
        ),
        out_specs=P(("groups", "dp", "sub"), "tensor"),
        check_vma=False,
    )
```

```python
import functools

import jax
import jax.numpy as jnp
from jax import lax
from jax.experimental import pallas as pl
from jax.experimental.pallas import tpu as pltpu
from jax.sharding import PartitionSpec as P

FEATURE_SHARES = (11, 11, 11, 11, 10, 10)
LANE_SHARES = (12, 12, 8)
QUEUE = 2
VMEM = 16 * 1024 * 1024
ANY = pl.BlockSpec(memory_space=pl.ANY)


def shifted(block, axis, distance):
    devices = range(lax.axis_size(axis))
    route = [((i - distance) % len(devices), i) for i in devices]
    return lax.ppermute(block, axis, route)


def mate(block):
    return shifted(block, "sub", 1)


def across(block):
    return shifted(block, "groups", 1)


def tied(value, *earlier):
    return lax.optimization_barrier((value, *earlier))[0] if earlier else value


def cuts(total, unit, shares):
    units, whole, done, marks = total // unit, sum(shares), 0, [0]
    for share in shares:
        done += share
        marks.append(units * done // whole * unit)
    marks[-1] = total
    return list(zip(marks[:-1], marks[1:]))


def call(kernel, operands, in_specs, out, out_spec, scratch, aliases):
    return pl.pallas_call(
        kernel,
        in_specs=in_specs,
        out_specs=out_spec,
        out_shape=out,
        scratch_shapes=scratch,
        input_output_aliases=aliases,
        compiler_params=pltpu.CompilerParams(vmem_limit_bytes=VMEM),
        cost_estimate=pl.CostEstimate(flops=1, bytes_accessed=1, transcendentals=0),
    )(*operands)


def products_kernel(sets, groups, spans, before, *refs):
    row_refs, unit_refs, total = refs[:sets], refs[sets : sets + groups * len(spans)], refs[-1]
    out = refs[-2]
    for step, (a, b) in enumerate(spans):
        units = jnp.concatenate(
            [ref[:, : b - a] for ref in unit_refs[step * groups : (step + 1) * groups]], axis=0
        )
        at = 0
        for ref in row_refs:
            spot = slice(at, at + ref.shape[0])
            at += ref.shape[0]
            value = lax.dot_general(
                ref[:, a:b], units, (((1,), (1,)), ((), ())), preferred_element_type=jnp.float32
            )
            if step > 0:
                value += total[spot]
            elif before:
                value += refs[-3][spot]
            if step < len(spans) - 1:
                total[spot] = value
            else:
                out[spot] = value.astype(out.dtype)


def products(row_sets, unit_sets, spans, before=None, out_type=jnp.bfloat16):
    groups = len(unit_sets) // len(spans)
    shape = (
        sum(r.shape[0] for r in row_sets),
        sum(u.shape[0] for u in unit_sets[:groups]),
    )
    operands = (*row_sets, *unit_sets)
    if before is not None:
        operands += (before,)
    whole = pl.BlockSpec(memory_space=pltpu.VMEM)
    return call(
        functools.partial(
            products_kernel, len(row_sets), groups, tuple(spans), before is not None
        ),
        operands,
        [whole] * len(operands),
        jax.ShapeDtypeStruct(shape, out_type),
        whole,
        [pltpu.VMEM(shape, jnp.float32)],
        {},
    )


def blocks_of(parts):
    found = []
    for i, (a, half, own, other) in enumerate(parts):
        arrays = [(0, lanes) for lanes in own] + [(1, lanes) for lanes in other]
        filled = [0, 0]
        for n, (k, lanes) in enumerate(arrays):
            for lane in range(0, lanes, 512):
                size = min(512, lanes - lane)
                turn = half - 2 * k * half if other else 0
                found.append((i, n, lane, size, (a + k * half + filled[k] + lane, turn)))
            filled[k] += lanes
    return found


def output_kernel(parts, side_ref, *refs):
    hidden, down = refs[:4], refs[4:6]
    arrived, at = [], 6
    for _, _, own, other in parts:
        count = len(own) + len(other)
        arrived.append((refs[at : at + count], refs[at + count : at + 2 * count]))
        at += 2 * count
    out, result, sems = refs[-3:]
    side = side_ref[0]
    stores, at = [], 0
    for n, (i, array, lane, size, (fixed, turn)) in enumerate(blocks_of(parts)):
        column = pl.ds(pl.multiple_of(fixed + side * turn, 128), size)
        spot = pl.ds(at, size)
        at += size
        total = None
        for m in range(4):
            if m < 2:
                weight = down[m][:, column]
            else:
                weight = arrived[i][m - 2][array][:, lane : lane + size]
            term = jnp.dot(hidden[m][...], weight, preferred_element_type=jnp.float32)
            total = term if total is None else total + term
        result[:, spot] = total.astype(result.dtype)
        stores.append(
            pltpu.make_async_copy(result.at[:, spot], out.at[:, column], sems.at[n])
        )
        stores[-1].start()
    for copy in stores:
        copy.wait()


def output_part(result, parts, side, hidden, down, arrived):
    rows, width = hidden[0].shape[0], down[0].shape[1]
    lanes = sum(sum(own) + sum(other) for _, _, own, other in parts)
    operands = [side, *hidden, *down, *arrived]
    in_specs = (
        [pl.BlockSpec(memory_space=pltpu.SMEM)]
        + [pl.BlockSpec(memory_space=pltpu.VMEM)] * (6 + len(arrived))
    )
    aliases = {}
    if result is not None:
        aliases = {len(operands): 0}
        operands.append(result)
        in_specs.append(ANY)
    return call(
        functools.partial(output_kernel, parts),
        operands,
        in_specs,
        jax.ShapeDtypeStruct((rows, width), jnp.bfloat16),
        ANY,
        [
            pltpu.VMEM((rows, lanes), jnp.bfloat16),
            pltpu.SemaphoreType.DMA((len(blocks_of(parts)),)),
        ],
        aliases,
    )


def over_slices(partial_value):
    return [
        shifted(partial_value, "tensor", distance)
        for distance in range(1, lax.axis_size("tensor"))
    ]


def summed(partial_value, sent):
    total = partial_value.astype(jnp.float32)
    for block in sent:
        total = total + block.astype(jnp.float32)
    return total


def gated(gate, up):
    return (jax.nn.silu(gate) * up).astype(jnp.bfloat16)


def on_device(tokens, gate_weight, up_weight, down_weight):
    units, width = gate_weight.shape
    rows = tokens.shape[0]
    group = lax.axis_index("groups").astype(jnp.int32)
    first = group == 0
    side = group.reshape(1)

    spans = cuts(width, 128, FEATURE_SHARES)
    lane_cuts = [(2 * a, 2 * b) for a, b in cuts(width // 2, 128, LANE_SHARES)]
    count = len(spans)
    total_count = count + len(lane_cuts)
    last = total_count - 1

    def piece(i, *after):
        if i < count:
            a, b = spans[i]
            gate, up = gate_weight, up_weight
            if after:
                gate, up = lax.optimization_barrier((gate, up, *after))[:2]
            return jnp.where(first, gate[:, a:b], up[:, a:b])
        a, b = lane_cuts[i - count]
        mid = (a + b) // 2
        down = tied(down_weight, *after)
        if i == last:
            return down[:, a:b]
        return jnp.where(first, down[:, a:mid], down[:, mid:b])

    pieces = [piece(0)]
    pieces.append(piece(1, pieces[0]))
    pieces += [piece(i, pieces[1]) for i in range(2, total_count)]
    waiting = [shifted(pieces[i], "dp", 1) for i in range(QUEUE)]
    landed, crossed, mates, crossed_mates = [], {}, {}, {}

    def advance(*after):
        i = len(landed)
        held = [*after, *landed[-1:]]
        held += [crossed[j] for j in range(count) if j + 2 == i]
        block = tied(waiting[i], *held)
        landed.append(block)
        if i < last:
            crossed[i] = across(block)
        if i + QUEUE < total_count:
            waiting.append(shifted(tied(pieces[i + QUEUE], block), "dp", 1))
        return block

    def pass_on(n, *after):
        i = count + n
        held = [tied(landed[i], *after)]
        if i < last:
            held.append(tied(crossed[i], *after))
        mates[i], *rest = [mate(block) for block in held]
        if rest:
            crossed_mates[i] = rest[0]

    def local(partial_value, sent):
        pre = summed(partial_value, sent)
        return gated(pre[:, :units], pre[:, units:])

    def batch(lo, hi, now, before=None, out_type=jnp.float32):
        held = [block for i in range(lo, hi) for block in (landed[i], crossed[i])]
        held = lax.optimization_barrier((*held, now))[:-1]
        return products([tokens, tokens_mate], held, spans[lo:hi], before, out_type)

    def activated(partial_value, sent):
        pre = summed(partial_value, sent)
        half = pre.shape[1] // 2
        left, right = pre[:, :half], pre[:, half:]
        return gated(jnp.where(first, left, right), jnp.where(first, right, left))

    tokens_mate = mate(tied(tokens, pieces[0]))
    down_mate = mate(tied(down_weight, pieces[1]))
    advance(*pieces[2:])
    now = advance(tokens_mate, down_mate)
    value = products(
        [tied(tokens, now), tokens_mate], [gate_weight, up_weight], [(0, width)]
    )
    now = advance(value)
    sent = over_slices(value)
    now = advance()
    now = advance()
    here = local(value, [tied(block, now) for block in sent])
    here_mate = mate(here[rows:])
    here = here[:rows]
    value = batch(0, 2, now)
    now = advance(value, here)
    value = batch(2, count - 1, now, value)
    now = advance(value, here_mate)
    value = batch(count - 1, count, now, value, jnp.bfloat16)
    halves = [value[:rows], value[rows:]]
    sent = [over_slices(half) for half in halves]
    now = advance(value)
    pass_on(0, now)
    there, given = (
        activated(half, [tied(block, now) for block in blocks])
        for half, blocks in zip(halves, sent)
    )
    there_mate = mate(given)

    def write(result, *which):
        parts, arrived = [], []
        for n in which:
            i = count + n
            a, b = lane_cuts[n]
            if i == last:
                parts.append((a, (b - a) // 2, (b - a,), ()))
                arrived += [landed[i], mates[i]]
            else:
                half = (b - a) // 2
                parts.append((a, half, (half,), (half,)))
                arrived += [landed[i], crossed[i], mates[i], crossed_mates[i]]
        return output_part(
            result,
            tuple(parts),
            side,
            [here, here_mate, there, there_mate],
            [down_weight, down_mate],
            arrived,
        )

    result = write(None, 0)
    pass_on(1, result)
    now = advance(result)
    pass_on(2, now)
    result = write(result, 1)
    return write(result, 2)


def solution(mesh):
    return jax.shard_map(
        on_device,
        mesh=mesh,
        in_specs=(
            P(("groups", "dp", "sub"), "tensor"),
            P(("dp", "sub"), "tensor"),
            P(("dp", "sub"), "tensor"),
            P(("dp", "sub"), "tensor"),
        ),
        out_specs=P(("groups", "dp", "sub"), "tensor"),
        check_vma=False,
    )
```

```python
import functools

import jax
import jax.numpy as jnp
from jax import lax
from jax.experimental import pallas as pl
from jax.experimental.pallas import tpu as pltpu
from jax.sharding import PartitionSpec as P

FEATURE_SHARES = (11, 11, 11, 11, 10, 10)
LANE_SHARES = (10, 9, 7, 6)
QUEUE = 2
VMEM = 16 * 1024 * 1024
ANY = pl.BlockSpec(memory_space=pl.ANY)


def shifted(block, axis, distance):
    devices = range(lax.axis_size(axis))
    route = [((i - distance) % len(devices), i) for i in devices]
    return lax.ppermute(block, axis, route)


def mate(block):
    return shifted(block, "sub", 1)


def across(block):
    return shifted(block, "groups", 1)


def tied(value, *earlier):
    return lax.optimization_barrier((value, *earlier))[0] if earlier else value


def cuts(total, unit, shares):
    units, whole, done, marks = total // unit, sum(shares), 0, [0]
    for share in shares:
        done += share
        marks.append(units * done // whole * unit)
    marks[-1] = total
    return list(zip(marks[:-1], marks[1:]))


def call(kernel, operands, in_specs, out, out_spec, scratch, aliases):
    return pl.pallas_call(
        kernel,
        in_specs=in_specs,
        out_specs=out_spec,
        out_shape=out,
        scratch_shapes=scratch,
        input_output_aliases=aliases,
        compiler_params=pltpu.CompilerParams(vmem_limit_bytes=VMEM),
        cost_estimate=pl.CostEstimate(flops=1, bytes_accessed=1, transcendentals=0),
    )(*operands)


def products_kernel(sets, groups, spans, before, *refs):
    row_refs, unit_refs, total = refs[:sets], refs[sets : sets + groups * len(spans)], refs[-1]
    out = refs[-2]
    for step, (a, b) in enumerate(spans):
        units = jnp.concatenate(
            [ref[:, : b - a] for ref in unit_refs[step * groups : (step + 1) * groups]], axis=0
        )
        at = 0
        for ref in row_refs:
            spot = slice(at, at + ref.shape[0])
            at += ref.shape[0]
            value = lax.dot_general(
                ref[:, a:b], units, (((1,), (1,)), ((), ())), preferred_element_type=jnp.float32
            )
            if step > 0:
                value += total[spot]
            elif before:
                value += refs[-3][spot]
            if step < len(spans) - 1:
                total[spot] = value
            else:
                out[spot] = value.astype(out.dtype)


def products(row_sets, unit_sets, spans, before=None, out_type=jnp.bfloat16):
    groups = len(unit_sets) // len(spans)
    shape = (
        sum(r.shape[0] for r in row_sets),
        sum(u.shape[0] for u in unit_sets[:groups]),
    )
    operands = (*row_sets, *unit_sets)
    if before is not None:
        operands += (before,)
    whole = pl.BlockSpec(memory_space=pltpu.VMEM)
    return call(
        functools.partial(
            products_kernel, len(row_sets), groups, tuple(spans), before is not None
        ),
        operands,
        [whole] * len(operands),
        jax.ShapeDtypeStruct(shape, out_type),
        whole,
        [pltpu.VMEM(shape, jnp.float32)],
        {},
    )


def blocks_of(parts):
    found = []
    for i, (a, lanes, half, others) in enumerate(parts):
        for lane in range(0, lanes, 512):
            size = min(512, lanes - lane)
            fixed = a + lane + (half if others else 0)
            found.append((i, lane, size, (fixed, -half if others else half)))
    return found


def output_kernel(parts, side_ref, *refs):
    hidden, down, arrived = refs[:4], refs[4:6], refs[6 : 6 + 2 * len(parts)]
    out, result, sems = refs[-3:]
    side = side_ref[0]
    stores, at = [], 0
    for n, (i, lane, size, (fixed, turn)) in enumerate(blocks_of(parts)):
        column = pl.ds(pl.multiple_of(fixed + side * turn, 128), size)
        spot = pl.ds(at, size)
        at += size
        total = None
        for m in range(4):
            if m < 2:
                weight = down[m][:, column]
            else:
                weight = arrived[2 * i + m - 2][:, lane : lane + size]
            term = jnp.dot(hidden[m][...], weight, preferred_element_type=jnp.float32)
            total = term if total is None else total + term
        result[:, spot] = total.astype(result.dtype)
        stores.append(
            pltpu.make_async_copy(result.at[:, spot], out.at[:, column], sems.at[n])
        )
        stores[-1].start()
    for copy in stores:
        copy.wait()


def output_part(result, parts, side, hidden, down, arrived):
    rows, width = hidden[0].shape[0], down[0].shape[1]
    lanes = sum(part[1] for part in parts)
    operands = [side, *hidden, *down, *arrived]
    in_specs = (
        [pl.BlockSpec(memory_space=pltpu.SMEM)]
        + [pl.BlockSpec(memory_space=pltpu.VMEM)] * (6 + len(arrived))
    )
    aliases = {}
    if result is not None:
        aliases = {len(operands): 0}
        operands.append(result)
        in_specs.append(ANY)
    return call(
        functools.partial(output_kernel, parts),
        operands,
        in_specs,
        jax.ShapeDtypeStruct((rows, width), jnp.bfloat16),
        ANY,
        [
            pltpu.VMEM((rows, lanes), jnp.bfloat16),
            pltpu.SemaphoreType.DMA((len(blocks_of(parts)),)),
        ],
        aliases,
    )


def over_slices(partial_value):
    return [
        shifted(partial_value, "tensor", distance)
        for distance in range(1, lax.axis_size("tensor"))
    ]


def summed(partial_value, sent):
    total = partial_value.astype(jnp.float32)
    for block in sent:
        total = total + block.astype(jnp.float32)
    return total


def gated(gate, up):
    return (jax.nn.silu(gate) * up).astype(jnp.bfloat16)


def on_device(tokens, gate_weight, up_weight, down_weight):
    units, width = gate_weight.shape
    rows = tokens.shape[0]
    group = lax.axis_index("groups").astype(jnp.int32)
    first = group == 0
    side = group.reshape(1)

    spans = cuts(width, 128, FEATURE_SHARES)
    lane_cuts = [(2 * a, 2 * b) for a, b in cuts(width // 2, 128, LANE_SHARES)]
    count = len(spans)
    total_count = count + len(lane_cuts)
    last = total_count - 1

    def piece(i, *after):
        if i < count:
            a, b = spans[i]
            gate, up = gate_weight, up_weight
            if after:
                gate, up = lax.optimization_barrier((gate, up, *after))[:2]
            return jnp.where(first, gate[:, a:b], up[:, a:b])
        a, b = lane_cuts[i - count]
        mid = (a + b) // 2
        down = tied(down_weight, *after)
        if i == last:
            return down[:, a:b]
        return jnp.where(first, down[:, a:mid], down[:, mid:b])

    pieces = [piece(0)]
    pieces.append(piece(1, pieces[0]))
    pieces += [piece(i, pieces[1]) for i in range(2, total_count)]
    waiting = [shifted(pieces[i], "dp", 1) for i in range(QUEUE)]
    landed, crossed, mates, crossed_mates = [], {}, {}, {}

    def advance(*after):
        i = len(landed)
        held = [*after, *landed[-1:]]
        held += [crossed[j] for j in range(count) if j + 2 == i]
        block = tied(waiting[i], *held)
        landed.append(block)
        if i < last:
            crossed[i] = across(block)
        if i + QUEUE < total_count:
            waiting.append(shifted(tied(pieces[i + QUEUE], block), "dp", 1))
        return block

    def pass_own(n, *after):
        mates[n] = mate(tied(landed[count + n], *after))

    def pass_other(n, *after):
        crossed_mates[n] = mate(tied(crossed[count + n], *after))

    def local(partial_value, sent):
        pre = summed(partial_value, sent)
        return gated(pre[:, :units], pre[:, units:])

    def batch(lo, hi, now, before=None, out_type=jnp.float32):
        held = [block for i in range(lo, hi) for block in (landed[i], crossed[i])]
        held = lax.optimization_barrier((*held, now))[:-1]
        return products([tokens, tokens_mate], held, spans[lo:hi], before, out_type)

    def activated(partial_value, sent):
        pre = summed(partial_value, sent)
        half = pre.shape[1] // 2
        left, right = pre[:, :half], pre[:, half:]
        return gated(jnp.where(first, left, right), jnp.where(first, right, left))

    tokens_mate = mate(tied(tokens, pieces[0]))
    down_mate = mate(tied(down_weight, pieces[1]))
    advance(*pieces[2:])
    now = advance(tokens_mate, down_mate)
    own_value = products(
        [tied(tokens, now), tokens_mate], [gate_weight, up_weight], [(0, width)]
    )
    now = advance(own_value)
    own_sent = over_slices(own_value)
    now = advance()
    value = batch(0, 2, now)
    now = advance(value)
    here = local(own_value, [tied(block, now) for block in own_sent])
    here_mate = mate(here[rows:])
    here = here[:rows]
    now = advance(here)
    value = batch(2, count - 1, now, value)
    now = advance(value, here_mate)
    value = batch(count - 1, count, now, value, jnp.bfloat16)
    halves = [value[:rows], value[rows:]]
    sent = [over_slices(half) for half in halves]
    now = advance(value)
    pass_own(0, now)
    now = advance(crossed[count])
    pass_own(1, now)
    pass_other(0, now)
    there, given = (
        activated(half, [tied(block, now) for block in blocks])
        for half, blocks in zip(halves, sent)
    )
    there_mate = tied(mate(given), crossed[count + 1])

    def write(result, *which):
        parts, arrived = [], []
        for n, others in which:
            a, b = lane_cuts[n]
            half = (b - a) // 2
            if count + n == last:
                parts.append((a, b - a, 0, False))
                arrived += [landed[last], mates[n]]
            elif others:
                parts.append((a, half, half, True))
                arrived += [crossed[count + n], crossed_mates[n]]
            else:
                parts.append((a, half, half, False))
                arrived += [landed[count + n], mates[n]]
        return output_part(
            result,
            tuple(parts),
            side,
            [here, here_mate, there, there_mate],
            [down_weight, down_mate],
            arrived,
        )

    result = write(None, (0, False), (0, True), (1, False))
    pass_own(2, result)
    pass_other(1, result)
    now = advance(result)
    pass_own(3, now)
    pass_other(2, now)
    result = write(result, (2, False), (1, True))
    result = write(result, (3, False))
    return write(result, (2, True))


def solution(mesh):
    return jax.shard_map(
        on_device,
        mesh=mesh,
        in_specs=(
            P(("groups", "dp", "sub"), "tensor"),
            P(("dp", "sub"), "tensor"),
            P(("dp", "sub"), "tensor"),
            P(("dp", "sub"), "tensor"),
        ),
        out_specs=P(("groups", "dp", "sub"), "tensor"),
        check_vma=False,
    )
```

```python
import functools

import jax
import jax.numpy as jnp
from jax import lax
from jax.experimental import pallas as pl
from jax.experimental.pallas import tpu as pltpu
from jax.sharding import PartitionSpec as P

FEATURE_SHARES = (1,) * 8
LANE_SHARES = (12, 12, 8)
QUEUE = 2
VMEM = 16 * 1024 * 1024
ANY = pl.BlockSpec(memory_space=pl.ANY)


def shifted(block, axis, distance):
    devices = range(lax.axis_size(axis))
    route = [((i - distance) % len(devices), i) for i in devices]
    return lax.ppermute(block, axis, route)


def mate(block):
    return shifted(block, "sub", 1)


def across(block):
    return shifted(block, "groups", 1)


def tied(value, *earlier):
    return lax.optimization_barrier((value, *earlier))[0] if earlier else value


def cuts(total, unit, shares):
    units, whole, done, marks = total // unit, sum(shares), 0, [0]
    for share in shares:
        done += share
        marks.append(units * done // whole * unit)
    marks[-1] = total
    return list(zip(marks[:-1], marks[1:]))


def call(kernel, operands, in_specs, out, out_spec, scratch, aliases):
    return pl.pallas_call(
        kernel,
        in_specs=in_specs,
        out_specs=out_spec,
        out_shape=out,
        scratch_shapes=scratch,
        input_output_aliases=aliases,
        compiler_params=pltpu.CompilerParams(vmem_limit_bytes=VMEM),
        cost_estimate=pl.CostEstimate(flops=1, bytes_accessed=1, transcendentals=0),
    )(*operands)


def products_kernel(sets, groups, spans, before, held, *refs):
    row_refs, unit_refs = refs[:sets], refs[sets : sets + groups * len(spans)]
    extra = 3 if held else 1
    out, total = refs[-1 - extra], refs[-extra]
    copies = []
    if held:
        rows, sems = refs[-2:]
        width = 0
        for step, (a, b) in enumerate(spans):
            at = 0
            for i, ref in enumerate(row_refs):
                copies.append(
                    pltpu.make_async_copy(
                        ref.at[:, a:b],
                        rows.at[at : at + ref.shape[0], width : width + b - a],
                        sems.at[step, i],
                    )
                )
                copies[-1].start()
                at += ref.shape[0]
            width += b - a
    width = 0
    for step, (a, b) in enumerate(spans):
        units = jnp.concatenate(
            [ref[:, : b - a] for ref in unit_refs[step * groups : (step + 1) * groups]], axis=0
        )
        at = 0
        for i, ref in enumerate(row_refs):
            spot = slice(at, at + ref.shape[0])
            at += ref.shape[0]
            if held:
                copies[step * sets + i].wait()
                block = rows[spot, width : width + b - a]
            else:
                block = ref[:, a:b]
            value = lax.dot_general(
                block, units, (((1,), (1,)), ((), ())), preferred_element_type=jnp.float32
            )
            if step > 0:
                value += total[spot]
            elif before:
                value += refs[-2 - extra][spot]
            if step < len(spans) - 1:
                total[spot] = value
            else:
                out[spot] = value.astype(out.dtype)
        width += b - a


def products(row_sets, unit_sets, spans, before=None, out_type=jnp.bfloat16, held=False):
    groups = len(unit_sets) // len(spans)
    shape = (
        sum(r.shape[0] for r in row_sets),
        sum(u.shape[0] for u in unit_sets[:groups]),
    )
    operands = (*row_sets, *unit_sets)
    if before is not None:
        operands += (before,)
    whole = pl.BlockSpec(memory_space=pltpu.VMEM)
    scratch = [pltpu.VMEM(shape, jnp.float32)]
    if held:
        scratch += [
            pltpu.VMEM((shape[0], sum(b - a for a, b in spans)), jnp.bfloat16),
            pltpu.SemaphoreType.DMA((len(spans), len(row_sets))),
        ]
    return call(
        functools.partial(
            products_kernel, len(row_sets), groups, tuple(spans), before is not None, held
        ),
        operands,
        [ANY if held else whole] * len(row_sets)
        + [whole] * (len(operands) - len(row_sets)),
        jax.ShapeDtypeStruct(shape, out_type),
        whole,
        scratch,
        {},
    )


def blocks_of(parts):
    found = []
    for i, (a, half, own, other) in enumerate(parts):
        arrays = [(0, lanes) for lanes in own] + [(1, lanes) for lanes in other]
        filled = [0, 0]
        for n, (k, lanes) in enumerate(arrays):
            for lane in range(0, lanes, 512):
                size = min(512, lanes - lane)
                turn = half - 2 * k * half if other else 0
                found.append((i, n, lane, size, (a + k * half + filled[k] + lane, turn)))
            filled[k] += lanes
    return found


def output_kernel(parts, side_ref, *refs):
    hidden, down = refs[:4], refs[4:6]
    arrived, at = [], 6
    for _, _, own, other in parts:
        count = len(own) + len(other)
        arrived.append((refs[at : at + count], refs[at + count : at + 2 * count]))
        at += 2 * count
    out, result, sems = refs[-3:]
    side = side_ref[0]
    stores, at = [], 0
    for n, (i, array, lane, size, (fixed, turn)) in enumerate(blocks_of(parts)):
        column = pl.ds(pl.multiple_of(fixed + side * turn, 128), size)
        spot = pl.ds(at, size)
        at += size
        total = None
        for m in range(4):
            if m < 2:
                weight = down[m][:, column]
            else:
                weight = arrived[i][m - 2][array][:, lane : lane + size]
            term = jnp.dot(hidden[m][...], weight, preferred_element_type=jnp.float32)
            total = term if total is None else total + term
        result[:, spot] = total.astype(result.dtype)
        stores.append(
            pltpu.make_async_copy(result.at[:, spot], out.at[:, column], sems.at[n])
        )
        stores[-1].start()
    for copy in stores:
        copy.wait()


def output_part(result, parts, side, hidden, down, arrived):
    rows, width = hidden[0].shape[0], down[0].shape[1]
    lanes = sum(sum(own) + sum(other) for _, _, own, other in parts)
    operands = [side, *hidden, *down, *arrived]
    in_specs = (
        [pl.BlockSpec(memory_space=pltpu.SMEM)]
        + [pl.BlockSpec(memory_space=pltpu.VMEM)] * (6 + len(arrived))
    )
    aliases = {}
    if result is not None:
        aliases = {len(operands): 0}
        operands.append(result)
        in_specs.append(ANY)
    return call(
        functools.partial(output_kernel, parts),
        operands,
        in_specs,
        jax.ShapeDtypeStruct((rows, width), jnp.bfloat16),
        ANY,
        [
            pltpu.VMEM((rows, lanes), jnp.bfloat16),
            pltpu.SemaphoreType.DMA((len(blocks_of(parts)),)),
        ],
        aliases,
    )


def over_slices(partial_value):
    return [
        shifted(partial_value, "tensor", distance)
        for distance in range(1, lax.axis_size("tensor"))
    ]


def summed(partial_value, sent):
    total = partial_value.astype(jnp.float32)
    for block in sent:
        total = total + block.astype(jnp.float32)
    return total


def gated(gate, up):
    return (jax.nn.silu(gate) * up).astype(jnp.bfloat16)


def on_device(tokens, gate_weight, up_weight, down_weight):
    units, width = gate_weight.shape
    rows = tokens.shape[0]
    group = lax.axis_index("groups").astype(jnp.int32)
    first = group == 0
    side = group.reshape(1)

    spans = cuts(width, 128, FEATURE_SHARES)
    lane_cuts = [(2 * a, 2 * b) for a, b in cuts(width // 2, 128, LANE_SHARES)]
    count = len(spans)
    total_count = count + len(lane_cuts)
    last = total_count - 1

    def piece(i, *after):
        if i < count:
            a, b = spans[i]
            gate, up = gate_weight, up_weight
            if after:
                gate, up = lax.optimization_barrier((gate, up, *after))[:2]
            return jnp.where(first, gate[:, a:b], up[:, a:b])
        a, b = lane_cuts[i - count]
        mid = (a + b) // 2
        down = tied(down_weight, *after)
        if i == last:
            return down[:, a:b]
        return jnp.where(first, down[:, a:mid], down[:, mid:b])

    pieces = [piece(0)]
    pieces.append(piece(1, pieces[0]))
    pieces += [piece(i, pieces[1]) for i in range(2, total_count)]
    waiting = [shifted(pieces[i], "dp", 1) for i in range(QUEUE)]
    landed, crossed, mates, crossed_mates = [], {}, {}, {}

    def advance(*after):
        i = len(landed)
        held = [*after, *landed[-1:]]
        held += [crossed[j] for j in range(count) if j + 2 == i]
        block = tied(waiting[i], *held)
        landed.append(block)
        if i < last:
            crossed[i] = across(block)
        if i + QUEUE < total_count:
            waiting.append(shifted(tied(pieces[i + QUEUE], block), "dp", 1))
        return block

    def pass_own(n, *after):
        mates[count + n] = mate(tied(landed[count + n], *after))

    def pass_other(n, *after):
        crossed_mates[count + n] = mate(tied(crossed[count + n], *after))

    def local(partial_value, sent):
        pre = summed(partial_value, sent)
        return gated(pre[:, :units], pre[:, units:])

    def batch(lo, hi, now, before=None, out_type=jnp.float32):
        held = [block for i in range(lo, hi) for block in (landed[i], crossed[i])]
        held = lax.optimization_barrier((*held, now))[:-1]
        return products([tokens, tokens_mate], held, spans[lo:hi], before, out_type, True)

    def activated(partial_value, sent):
        pre = summed(partial_value, sent)
        half = pre.shape[1] // 2
        left, right = pre[:, :half], pre[:, half:]
        return gated(jnp.where(first, left, right), jnp.where(first, right, left))

    tokens_mate = mate(tied(tokens, pieces[0]))
    down_mate = mate(tied(down_weight, pieces[1]))
    advance(*pieces[2:])
    advance()
    now = advance(tokens_mate, down_mate)
    own_value = products(
        [tied(tokens, now), tokens_mate], [gate_weight, up_weight], [(0, width)]
    )
    now = advance(own_value)
    own_sent = over_slices(own_value)
    advance()
    now = advance()
    value = batch(0, 4, now)
    now = advance(value)
    here = local(own_value, [tied(block, now) for block in own_sent])
    here_mate = mate(here[rows:])
    here = here[:rows]
    now = advance(here)
    value = batch(4, count - 1, now, value)
    now = advance(value, here_mate)
    value = batch(count - 1, count, now, value, jnp.bfloat16)
    halves = [value[:rows], value[rows:]]
    sent = [over_slices(half) for half in halves]
    now = advance(value)
    pass_own(0, now)
    pass_other(0, now)
    there, given = (
        activated(half, [tied(block, now) for block in blocks])
        for half, blocks in zip(halves, sent)
    )
    there_mate = mate(given)

    def write(result, *which):
        parts, arrived = [], []
        for n in which:
            i = count + n
            a, b = lane_cuts[n]
            if i == last:
                parts.append((a, (b - a) // 2, (b - a,), ()))
                arrived += [landed[i], mates[i]]
            else:
                half = (b - a) // 2
                parts.append((a, half, (half,), (half,)))
                arrived += [landed[i], crossed[i], mates[i], crossed_mates[i]]
        return output_part(
            result,
            tuple(parts),
            side,
            [here, here_mate, there, there_mate],
            [down_weight, down_mate],
            arrived,
        )

    result = write(None, 0)
    pass_own(1, result)
    pass_other(1, result)
    now = advance(result, crossed[count + 1])
    pass_own(2, now)
    result = write(result, 1)
    return write(result, 2)


def solution(mesh):
    return jax.shard_map(
        on_device,
        mesh=mesh,
        in_specs=(
            P(("groups", "dp", "sub"), "tensor"),
            P(("dp", "sub"), "tensor"),
            P(("dp", "sub"), "tensor"),
            P(("dp", "sub"), "tensor"),
        ),
        out_specs=P(("groups", "dp", "sub"), "tensor"),
        check_vma=False,
    )
```

```python
import functools

import jax
import jax.numpy as jnp
from jax import lax
from jax.experimental import pallas as pl
from jax.experimental.pallas import tpu as pltpu
from jax.sharding import PartitionSpec as P

FEATURE_SHARES = (1,) * 8
LANE_SHARES = (10, 12, 10)
QUEUE = 2
OWN, OWN_SUM, OWN_MATE = 1, 4, 6
BATCHES = ((5, 0, 4), (7, 4, 7), (8, 7, 8))
PASS = (9, 9)
BEFORE_LAST = (1, 0, 0)
WHOLE_FIRST = True
SWAP_WAIT = 2
SPLIT = False
HOLD = 1
VMEM = 16 * 1024 * 1024
ANY = pl.BlockSpec(memory_space=pl.ANY)


def shifted(block, axis, distance):
    devices = range(lax.axis_size(axis))
    route = [((i - distance) % len(devices), i) for i in devices]
    return lax.ppermute(block, axis, route)


def mate(block):
    return shifted(block, "sub", 1)


def across(block):
    return shifted(block, "groups", 1)


def tied(value, *earlier):
    return lax.optimization_barrier((value, *earlier))[0] if earlier else value


def cuts(total, unit, shares):
    units, whole, done, marks = total // unit, sum(shares), 0, [0]
    for share in shares:
        done += share
        marks.append(units * done // whole * unit)
    marks[-1] = total
    return list(zip(marks[:-1], marks[1:]))


def call(kernel, operands, in_specs, out, out_spec, scratch, aliases):
    return pl.pallas_call(
        kernel,
        in_specs=in_specs,
        out_specs=out_spec,
        out_shape=out,
        scratch_shapes=scratch,
        input_output_aliases=aliases,
        compiler_params=pltpu.CompilerParams(vmem_limit_bytes=VMEM),
        cost_estimate=pl.CostEstimate(flops=1, bytes_accessed=1, transcendentals=0),
    )(*operands)


def products_kernel(sets, groups, spans, before, outs, *refs):
    row_refs, unit_refs = refs[:sets], refs[sets : sets + groups * len(spans)]
    out_refs, total = refs[-1 - outs : -1], refs[-1]
    for step, (a, b) in enumerate(spans):
        units = jnp.concatenate(
            [ref[:, : b - a] for ref in unit_refs[step * groups : (step + 1) * groups]], axis=0
        )
        at = 0
        for i, ref in enumerate(row_refs):
            spot = slice(at, at + ref.shape[0])
            at += ref.shape[0]
            value = lax.dot_general(
                ref[:, a:b], units, (((1,), (1,)), ((), ())), preferred_element_type=jnp.float32
            )
            if step > 0:
                value += total[spot]
            elif before:
                value += refs[-2 - outs][spot]
            if step < len(spans) - 1:
                total[spot] = value
            elif outs == 1:
                out_refs[0][spot] = value.astype(out_refs[0].dtype)
            else:
                out_refs[i][...] = value.astype(out_refs[i].dtype)


WHOLE = pl.BlockSpec(memory_space=pltpu.VMEM)


def products(row_sets, unit_sets, spans, before=None, out_type=jnp.bfloat16, split=False):
    groups = len(unit_sets) // len(spans)
    count = sum(u.shape[0] for u in unit_sets[:groups])
    shape = (sum(r.shape[0] for r in row_sets), count)
    shapes = [(r.shape[0], count) for r in row_sets] if split else [shape]
    operands = (*row_sets, *unit_sets)
    if before is not None:
        operands += (before,)
    found = call(
        functools.partial(
            products_kernel, len(row_sets), groups, tuple(spans), before is not None, len(shapes)
        ),
        operands,
        [WHOLE] * len(operands),
        [jax.ShapeDtypeStruct(s, out_type) for s in shapes],
        [WHOLE] * len(shapes),
        [pltpu.VMEM(shape, jnp.float32)],
        {},
    )
    return found if split else found[0]


def activation_kernel(count, turned, side_ref, *refs):
    terms, outs = refs[:-2], refs[-2:]
    per = len(terms) // count
    rows, units = outs[0].shape
    first = side_ref[0] == 0
    at = 0
    for i in range(count):
        block = terms[i * per : (i + 1) * per]
        for start in range(0, block[0].shape[0], rows):
            total = block[0][start : start + rows].astype(jnp.float32)
            for ref in block[1:]:
                total += ref[start : start + rows].astype(jnp.float32)
            gate, up = total[:, :units], total[:, units:]
            if turned:
                gate, up = jnp.where(first, gate, up), jnp.where(first, up, gate)
            outs[at][...] = (gate / (1.0 + jnp.exp(-gate)) * up).astype(outs[at].dtype)
            at += 1


def activated(side, blocks, rows, turned):
    operands = [side]
    for value, others in blocks:
        operands += [value, *others]
    shape = (rows, blocks[0][0].shape[1] // 2)
    return call(
        functools.partial(activation_kernel, len(blocks), turned),
        operands,
        [pl.BlockSpec(memory_space=pltpu.SMEM)] + [WHOLE] * (len(operands) - 1),
        [jax.ShapeDtypeStruct(shape, jnp.bfloat16)] * 2,
        [WHOLE] * 2,
        [],
        {},
    )


def blocks_of(parts):
    found = []
    for i, (a, half, own, other) in enumerate(parts):
        arrays = [(0, lanes) for lanes in own] + [(1, lanes) for lanes in other]
        filled = [0, 0]
        for n, (k, lanes) in enumerate(arrays):
            for lane in range(0, lanes, 512):
                size = min(512, lanes - lane)
                turn = half - 2 * k * half if other else 0
                found.append((i, n, lane, size, (a + k * half + filled[k] + lane, turn)))
            filled[k] += lanes
    return found


def output_kernel(parts, side_ref, *refs):
    hidden, down = refs[:4], refs[4:6]
    arrived, at = [], 6
    for _, _, own, other in parts:
        count = len(own) + len(other)
        arrived.append((refs[at : at + count], refs[at + count : at + 2 * count]))
        at += 2 * count
    out, result, sems = refs[-3:]
    side = side_ref[0]
    stores, at = [], 0
    for n, (i, array, lane, size, (fixed, turn)) in enumerate(blocks_of(parts)):
        column = pl.ds(pl.multiple_of(fixed + side * turn, 128), size)
        spot = pl.ds(at, size)
        at += size
        total = None
        for m in range(4):
            if m < 2:
                weight = down[m][:, column]
            else:
                weight = arrived[i][m - 2][array][:, lane : lane + size]
            term = jnp.dot(hidden[m][...], weight, preferred_element_type=jnp.float32)
            total = term if total is None else total + term
        result[:, spot] = total.astype(result.dtype)
        stores.append(
            pltpu.make_async_copy(result.at[:, spot], out.at[:, column], sems.at[n])
        )
        stores[-1].start()
    for copy in stores:
        copy.wait()


def output_part(result, parts, side, hidden, down, arrived):
    rows, width = hidden[0].shape[0], down[0].shape[1]
    lanes = sum(sum(own) + sum(other) for _, _, own, other in parts)
    operands = [side, *hidden, *down, *arrived]
    in_specs = (
        [pl.BlockSpec(memory_space=pltpu.SMEM)]
        + [pl.BlockSpec(memory_space=pltpu.VMEM)] * (6 + len(arrived))
    )
    aliases = {}
    if result is not None:
        aliases = {len(operands): 0}
        operands.append(result)
        in_specs.append(ANY)
    return call(
        functools.partial(output_kernel, parts),
        operands,
        in_specs,
        jax.ShapeDtypeStruct((rows, width), jnp.bfloat16),
        ANY,
        [
            pltpu.VMEM((rows, lanes), jnp.bfloat16),
            pltpu.SemaphoreType.DMA((len(blocks_of(parts)),)),
        ],
        aliases,
    )


def over_slices(partial_value):
    return [
        shifted(partial_value, "tensor", distance)
        for distance in range(1, lax.axis_size("tensor"))
    ]


def on_device(tokens, gate_weight, up_weight, down_weight):
    units, width = gate_weight.shape
    rows = tokens.shape[0]
    group = lax.axis_index("groups").astype(jnp.int32)
    first = group == 0
    side = group.reshape(1)

    spans = cuts(width, 128, FEATURE_SHARES)
    lane_cuts = [(2 * a, 2 * b) for a, b in cuts(width // 2, 128, LANE_SHARES)]
    count = len(spans)
    total_count = count + len(lane_cuts)
    last = total_count - 1

    def piece(i, *after):
        if i < count:
            a, b = spans[i]
            gate, up = gate_weight, up_weight
            if after:
                gate, up = lax.optimization_barrier((gate, up, *after))[:2]
            return jnp.where(first, gate[:, a:b], up[:, a:b])
        a, b = lane_cuts[i - count]
        mid = (a + b) // 2
        down = tied(down_weight, *after)
        if i == last:
            return down[:, a:b]
        return jnp.where(first, down[:, a:mid], down[:, mid:b])

    pieces = [piece(0)]
    pieces.append(piece(1, pieces[0]))
    pieces += [piece(i, pieces[1]) for i in range(2, total_count)]
    waiting = [shifted(pieces[i], "dp", 1) for i in range(QUEUE)]
    landed, crossed, mates, crossed_mates = [], {}, {}, {}

    def advance(*after):
        i = len(landed)
        held = [*after, *landed[-1:]]
        held += [crossed[j] for j in range(count) if j + SWAP_WAIT == i]
        block = tied(waiting[i], *held)
        landed.append(block)
        if i < last:
            crossed[i] = across(block)
        if i + QUEUE < total_count:
            waiting.append(shifted(tied(pieces[i + QUEUE], block), "dp", 1))
        return block

    def pass_own(n, *after):
        mates[count + n] = mate(tied(landed[count + n], *after))

    def pass_other(n, *after):
        crossed_mates[count + n] = mate(tied(crossed[count + n], *after))

    def batch(lo, hi, now, before=None, last_one=False):
        held = [block for i in range(lo, hi) for block in (landed[i], crossed[i])]
        held = lax.optimization_barrier((*held, now))[:-1]
        return products(
            [tokens, tokens_mate],
            held,
            spans[lo:hi],
            before,
            jnp.bfloat16 if last_one else jnp.float32,
            last_one and SPLIT,
        )

    tokens_mate = mate(tied(tokens, pieces[0]))
    down_mate = mate(tied(down_weight, pieces[1]))
    due = {0: pieces[2:], OWN: [tokens_mate, down_mate]}
    value = own_value = None
    for i in range(last):
        now = advance(*due.get(i, []))
        after = due.setdefault(i + 1, [])
        if i == OWN:
            own_value = products(
                [tied(tokens, now), tokens_mate], [gate_weight, up_weight], [(0, width)]
            )
            own_sent = over_slices(own_value)
            after.append(own_value)
        if i == OWN_SUM:
            here, given = activated(
                side, [(own_value, [tied(block, now) for block in own_sent])], rows, False
            )
            here_mate = mate(given)
            after.append(here)
            due.setdefault(OWN_MATE, []).append(here_mate)
        for stage, lo, hi in BATCHES:
            if i == stage:
                value = batch(lo, hi, now, value, hi == count)
                halves = value if isinstance(value, (list, tuple)) else [value]
                after += halves
                if hi == count:
                    sent = [over_slices(half) for half in halves]
        if i == PASS[0]:
            pass_own(0, now)
        if i == PASS[1]:
            pass_other(0, now)
    there, given = activated(
        side,
        [
            (half, [tied(block, now) for block in blocks])
            for half, blocks in zip(halves, sent)
        ],
        rows,
        True,
    )
    there_mate = mate(given)
    if HOLD:
        there_mate = tied(there_mate, crossed[count + 1])

    def write(result, *which):
        parts, arrived = [], []
        for n in which:
            i = count + n
            a, b = lane_cuts[n]
            if i == last:
                parts.append((a, (b - a) // 2, (b - a,), ()))
                arrived += [landed[i], mates[i]]
            else:
                half = (b - a) // 2
                parts.append((a, half, (half,), (half,)))
                arrived += [landed[i], crossed[i], mates[i], crossed_mates[i]]
        return output_part(
            result,
            tuple(parts),
            side,
            [here, here_mate, there, there_mate],
            [down_weight, down_mate],
            arrived,
        )

    result = write(None, 0)
    pass_own(1, result)
    pass_other(1, result)
    waits = (crossed[count + 1], mates[count + 1], crossed_mates[count + 1])
    now = advance(result, *(wait for wait, use in zip(waits, BEFORE_LAST) if use))
    pass_own(2, now)
    for n in (2, 1) if WHOLE_FIRST else (1, 2):
        result = write(result, n)
    return result


def solution(mesh):
    return jax.shard_map(
        on_device,
        mesh=mesh,
        in_specs=(
            P(("groups", "dp", "sub"), "tensor"),
            P(("dp", "sub"), "tensor"),
            P(("dp", "sub"), "tensor"),
            P(("dp", "sub"), "tensor"),
        ),
        out_specs=P(("groups", "dp", "sub"), "tensor"),
        check_vma=False,
    )
```

```python
import functools

import jax
import jax.numpy as jnp
from jax import lax
from jax.experimental import pallas as pl
from jax.experimental.pallas import tpu as pltpu
from jax.sharding import PartitionSpec as P

FEATURE_SHARES = (1,) * 8
LANE_SHARES = (10, 12, 10)
QUEUE = 2
OWN, OWN_SUM, OWN_MATE = 1, 4, 6
BATCHES = ((5, 0, 4), (7, 4, 7), (8, 7, 8))
PASS = (9, 9)
BEFORE_LAST = (1, 0, 0)
WHOLE_FIRST = True
SWAP_WAIT = 2
HOLD = 1
VMEM = 16 * 1024 * 1024
ANY = pl.BlockSpec(memory_space=pl.ANY)


def shifted(block, axis, distance):
    devices = range(lax.axis_size(axis))
    route = [((i - distance) % len(devices), i) for i in devices]
    return lax.ppermute(block, axis, route)


def mate(block):
    return shifted(block, "sub", 1)


def across(block):
    return shifted(block, "groups", 1)


def tied(value, *earlier):
    return lax.optimization_barrier((value, *earlier))[0] if earlier else value


def cuts(total, unit, shares):
    units, whole, done, marks = total // unit, sum(shares), 0, [0]
    for share in shares:
        done += share
        marks.append(units * done // whole * unit)
    marks[-1] = total
    return list(zip(marks[:-1], marks[1:]))


def call(kernel, operands, in_specs, out, out_spec, scratch, aliases):
    return pl.pallas_call(
        kernel,
        in_specs=in_specs,
        out_specs=out_spec,
        out_shape=out,
        scratch_shapes=scratch,
        input_output_aliases=aliases,
        compiler_params=pltpu.CompilerParams(vmem_limit_bytes=VMEM),
        cost_estimate=pl.CostEstimate(flops=1, bytes_accessed=1, transcendentals=0),
    )(*operands)


def products_kernel(sets, groups, spans, before, *refs):
    row_refs, unit_refs = refs[:sets], refs[sets : sets + groups * len(spans)]
    out, total = refs[-2:]
    for step, (a, b) in enumerate(spans):
        units = jnp.concatenate(
            [ref[:, : b - a] for ref in unit_refs[step * groups : (step + 1) * groups]], axis=0
        )
        rows = jnp.concatenate([ref[:, a:b] for ref in row_refs], axis=0)
        value = lax.dot_general(
            units, rows, (((1,), (1,)), ((), ())), preferred_element_type=jnp.float32
        )
        if step > 0:
            value += total[...]
        elif before:
            value += refs[-3][...]
        if step < len(spans) - 1:
            total[...] = value
        else:
            out[...] = value.astype(out.dtype)


WHOLE = pl.BlockSpec(memory_space=pltpu.VMEM)


def products(row_sets, unit_sets, spans, before=None, out_type=jnp.bfloat16):
    groups = len(unit_sets) // len(spans)
    shape = (sum(u.shape[0] for u in unit_sets[:groups]), sum(r.shape[0] for r in row_sets))
    operands = (*row_sets, *unit_sets)
    if before is not None:
        operands += (before,)
    return call(
        functools.partial(
            products_kernel, len(row_sets), groups, tuple(spans), before is not None
        ),
        operands,
        [WHOLE] * len(operands),
        jax.ShapeDtypeStruct(shape, out_type),
        WHOLE,
        [pltpu.VMEM(shape, jnp.float32)],
        {},
    )


def activation_kernel(turned, side_ref, *refs):
    terms, outs = refs[:-2], refs[-2:]
    rows, units = outs[0].shape
    total = terms[0][...].astype(jnp.float32)
    for ref in terms[1:]:
        total += ref[...].astype(jnp.float32)
    gate, up = total[:units], total[units:]
    if turned:
        first = side_ref[0] == 0
        gate, up = jnp.where(first, gate, up), jnp.where(first, up, gate)
    hidden = (gate / (1.0 + jnp.exp(-gate)) * up).T
    for i, out in enumerate(outs):
        out[...] = hidden[i * rows : (i + 1) * rows].astype(out.dtype)


def activated(side, value, others, turned):
    operands = [side, value, *others]
    shape = (value.shape[1] // 2, value.shape[0] // 2)
    return call(
        functools.partial(activation_kernel, turned),
        operands,
        [pl.BlockSpec(memory_space=pltpu.SMEM)] + [WHOLE] * (len(operands) - 1),
        [jax.ShapeDtypeStruct(shape, jnp.bfloat16)] * 2,
        [WHOLE] * 2,
        [],
        {},
    )


def blocks_of(parts):
    found = []
    for i, (a, half, own, other) in enumerate(parts):
        arrays = [(0, lanes) for lanes in own] + [(1, lanes) for lanes in other]
        filled = [0, 0]
        for n, (k, lanes) in enumerate(arrays):
            for lane in range(0, lanes, 512):
                size = min(512, lanes - lane)
                turn = half - 2 * k * half if other else 0
                found.append((i, n, lane, size, (a + k * half + filled[k] + lane, turn)))
            filled[k] += lanes
    return found


def output_kernel(parts, side_ref, *refs):
    hidden, down = refs[:4], refs[4:6]
    arrived, at = [], 6
    for _, _, own, other in parts:
        count = len(own) + len(other)
        arrived.append((refs[at : at + count], refs[at + count : at + 2 * count]))
        at += 2 * count
    out, result, sems = refs[-3:]
    side = side_ref[0]
    stores, at = [], 0
    for n, (i, array, lane, size, (fixed, turn)) in enumerate(blocks_of(parts)):
        column = pl.ds(pl.multiple_of(fixed + side * turn, 128), size)
        spot = pl.ds(at, size)
        at += size
        total = None
        for m in range(4):
            if m < 2:
                weight = down[m][:, column]
            else:
                weight = arrived[i][m - 2][array][:, lane : lane + size]
            term = jnp.dot(hidden[m][...], weight, preferred_element_type=jnp.float32)
            total = term if total is None else total + term
        result[:, spot] = total.astype(result.dtype)
        stores.append(
            pltpu.make_async_copy(result.at[:, spot], out.at[:, column], sems.at[n])
        )
        stores[-1].start()
    for copy in stores:
        copy.wait()


def output_part(result, parts, side, hidden, down, arrived):
    rows, width = hidden[0].shape[0], down[0].shape[1]
    lanes = sum(sum(own) + sum(other) for _, _, own, other in parts)
    operands = [side, *hidden, *down, *arrived]
    in_specs = (
        [pl.BlockSpec(memory_space=pltpu.SMEM)]
        + [pl.BlockSpec(memory_space=pltpu.VMEM)] * (6 + len(arrived))
    )
    aliases = {}
    if result is not None:
        aliases = {len(operands): 0}
        operands.append(result)
        in_specs.append(ANY)
    return call(
        functools.partial(output_kernel, parts),
        operands,
        in_specs,
        jax.ShapeDtypeStruct((rows, width), jnp.bfloat16),
        ANY,
        [
            pltpu.VMEM((rows, lanes), jnp.bfloat16),
            pltpu.SemaphoreType.DMA((len(blocks_of(parts)),)),
        ],
        aliases,
    )


def over_slices(partial_value):
    return [
        shifted(partial_value, "tensor", distance)
        for distance in range(1, lax.axis_size("tensor"))
    ]


def on_device(tokens, gate_weight, up_weight, down_weight):
    units, width = gate_weight.shape
    group = lax.axis_index("groups").astype(jnp.int32)
    first = group == 0
    side = group.reshape(1)

    spans = cuts(width, 128, FEATURE_SHARES)
    lane_cuts = [(2 * a, 2 * b) for a, b in cuts(width // 2, 128, LANE_SHARES)]
    count = len(spans)
    total_count = count + len(lane_cuts)
    last = total_count - 1

    def piece(i, *after):
        if i < count:
            a, b = spans[i]
            gate, up = gate_weight, up_weight
            if after:
                gate, up = lax.optimization_barrier((gate, up, *after))[:2]
            return jnp.where(first, gate[:, a:b], up[:, a:b])
        a, b = lane_cuts[i - count]
        mid = (a + b) // 2
        down = tied(down_weight, *after)
        if i == last:
            return down[:, a:b]
        return jnp.where(first, down[:, a:mid], down[:, mid:b])

    pieces = [piece(0)]
    pieces.append(piece(1, pieces[0]))
    pieces += [piece(i, pieces[1]) for i in range(2, total_count)]
    waiting = [shifted(pieces[i], "dp", 1) for i in range(QUEUE)]
    landed, crossed, mates, crossed_mates = [], {}, {}, {}

    def advance(*after):
        i = len(landed)
        held = [*after, *landed[-1:]]
        held += [crossed[j] for j in range(count) if j + SWAP_WAIT == i]
        block = tied(waiting[i], *held)
        landed.append(block)
        if i < last:
            crossed[i] = across(block)
        if i + QUEUE < total_count:
            waiting.append(shifted(tied(pieces[i + QUEUE], block), "dp", 1))
        return block

    def pass_own(n, *after):
        mates[count + n] = mate(tied(landed[count + n], *after))

    def pass_other(n, *after):
        crossed_mates[count + n] = mate(tied(crossed[count + n], *after))

    def batch(lo, hi, now, before=None):
        held = [block for i in range(lo, hi) for block in (landed[i], crossed[i])]
        held = lax.optimization_barrier((*held, now))[:-1]
        kind = jnp.bfloat16 if hi == count else jnp.float32
        return products([tokens, tokens_mate], held, spans[lo:hi], before, kind)

    tokens_mate = mate(tied(tokens, pieces[0]))
    down_mate = mate(tied(down_weight, pieces[1]))
    due = {0: pieces[2:], OWN: [tokens_mate, down_mate]}
    value = own_value = None
    for i in range(last):
        now = advance(*due.get(i, []))
        after = due.setdefault(i + 1, [])
        if i == OWN:
            own_value = products(
                [tied(tokens, now), tokens_mate], [gate_weight, up_weight], [(0, width)]
            )
            own_sent = over_slices(own_value)
            after.append(own_value)
        if i == OWN_SUM:
            here, given = activated(
                side, own_value, [tied(block, now) for block in own_sent], False
            )
            here_mate = mate(given)
            after.append(here)
            due.setdefault(OWN_MATE, []).append(here_mate)
        for stage, lo, hi in BATCHES:
            if i == stage:
                value = batch(lo, hi, now, value)
                after.append(value)
                if hi == count:
                    sent = over_slices(value)
        if i == PASS[0]:
            pass_own(0, now)
        if i == PASS[1]:
            pass_other(0, now)
    there, given = activated(side, value, [tied(block, now) for block in sent], True)
    there_mate = mate(given)
    if HOLD:
        there_mate = tied(there_mate, crossed[count + 1])

    def write(result, *which):
        parts, arrived = [], []
        for n in which:
            i = count + n
            a, b = lane_cuts[n]
            if i == last:
                parts.append((a, (b - a) // 2, (b - a,), ()))
                arrived += [landed[i], mates[i]]
            else:
                half = (b - a) // 2
                parts.append((a, half, (half,), (half,)))
                arrived += [landed[i], crossed[i], mates[i], crossed_mates[i]]
        return output_part(
            result,
            tuple(parts),
            side,
            [here, here_mate, there, there_mate],
            [down_weight, down_mate],
            arrived,
        )

    result = write(None, 0)
    pass_own(1, result)
    pass_other(1, result)
    waits = (crossed[count + 1], mates[count + 1], crossed_mates[count + 1])
    now = advance(result, *(wait for wait, use in zip(waits, BEFORE_LAST) if use))
    pass_own(2, now)
    for n in (2, 1) if WHOLE_FIRST else (1, 2):
        result = write(result, n)
    return result


def solution(mesh):
    return jax.shard_map(
        on_device,
        mesh=mesh,
        in_specs=(
            P(("groups", "dp", "sub"), "tensor"),
            P(("dp", "sub"), "tensor"),
            P(("dp", "sub"), "tensor"),
            P(("dp", "sub"), "tensor"),
        ),
        out_specs=P(("groups", "dp", "sub"), "tensor"),
        check_vma=False,
    )
```

```python
import functools

import jax
import jax.numpy as jnp
from jax import lax
from jax.experimental import pallas as pl
from jax.experimental.pallas import tpu as pltpu
from jax.sharding import PartitionSpec as P

FEATURE_SHARES = (1,) * 8
LANE_SHARES = (10, 13, 9)
WHOLES = 1
QUEUE = 2
OWN, OWN_SUM, OWN_MATE = 1, 4, 6
BATCHES = ((5, 0, 4), (7, 4, 7), (8, 7, 8))
PASS = (8, 9)
TAIL = (("own", 1), ("write", 0, -1, 1), ("other", 1), ("last", 1), ("write", 2), ("write", -2))
SWAP_WAIT = 2
HOLD = 0
VMEM = 16 * 1024 * 1024
ANY = pl.BlockSpec(memory_space=pl.ANY)


def shifted(block, axis, distance):
    devices = range(lax.axis_size(axis))
    route = [((i - distance) % len(devices), i) for i in devices]
    return lax.ppermute(block, axis, route)


def mate(block):
    return shifted(block, "sub", 1)


def across(block):
    return shifted(block, "groups", 1)


def tied(value, *earlier):
    return lax.optimization_barrier((value, *earlier))[0] if earlier else value


def cuts(total, unit, shares):
    units, whole, done, marks = total // unit, sum(shares), 0, [0]
    for share in shares:
        done += share
        marks.append(units * done // whole * unit)
    marks[-1] = total
    return list(zip(marks[:-1], marks[1:]))


def call(kernel, operands, in_specs, out, out_spec, scratch, aliases):
    return pl.pallas_call(
        kernel,
        in_specs=in_specs,
        out_specs=out_spec,
        out_shape=out,
        scratch_shapes=scratch,
        input_output_aliases=aliases,
        compiler_params=pltpu.CompilerParams(vmem_limit_bytes=VMEM),
        cost_estimate=pl.CostEstimate(flops=1, bytes_accessed=1, transcendentals=0),
    )(*operands)


def products_kernel(sets, groups, spans, before, *refs):
    row_refs, unit_refs = refs[:sets], refs[sets : sets + groups * len(spans)]
    out, total = refs[-2:]
    for step, (a, b) in enumerate(spans):
        units = jnp.concatenate(
            [ref[:, : b - a] for ref in unit_refs[step * groups : (step + 1) * groups]], axis=0
        )
        rows = jnp.concatenate([ref[:, a:b] for ref in row_refs], axis=0)
        value = lax.dot_general(
            units, rows, (((1,), (1,)), ((), ())), preferred_element_type=jnp.float32
        )
        if step > 0:
            value += total[...]
        elif before:
            value += refs[-3][...]
        if step < len(spans) - 1:
            total[...] = value
        else:
            out[...] = value.astype(out.dtype)


WHOLE = pl.BlockSpec(memory_space=pltpu.VMEM)


def products(row_sets, unit_sets, spans, before=None, out_type=jnp.bfloat16):
    groups = len(unit_sets) // len(spans)
    shape = (sum(u.shape[0] for u in unit_sets[:groups]), sum(r.shape[0] for r in row_sets))
    operands = (*row_sets, *unit_sets)
    if before is not None:
        operands += (before,)
    return call(
        functools.partial(
            products_kernel, len(row_sets), groups, tuple(spans), before is not None
        ),
        operands,
        [WHOLE] * len(operands),
        jax.ShapeDtypeStruct(shape, out_type),
        WHOLE,
        [pltpu.VMEM(shape, jnp.float32)],
        {},
    )


def activation_kernel(turned, side_ref, *refs):
    terms, outs = refs[:-2], refs[-2:]
    rows, units = outs[0].shape
    total = terms[0][...].astype(jnp.float32)
    for ref in terms[1:]:
        total += ref[...].astype(jnp.float32)
    gate, up = total[:units], total[units:]
    if turned:
        first = side_ref[0] == 0
        gate, up = jnp.where(first, gate, up), jnp.where(first, up, gate)
    hidden = (gate / (1.0 + jnp.exp(-gate)) * up).T
    for i, out in enumerate(outs):
        out[...] = hidden[i * rows : (i + 1) * rows].astype(out.dtype)


def activated(side, value, others, turned):
    operands = [side, value, *others]
    shape = (value.shape[1] // 2, value.shape[0] // 2)
    return call(
        functools.partial(activation_kernel, turned),
        operands,
        [pl.BlockSpec(memory_space=pltpu.SMEM)] + [WHOLE] * (len(operands) - 1),
        [jax.ShapeDtypeStruct(shape, jnp.bfloat16)] * 2,
        [WHOLE] * 2,
        [],
        {},
    )


def blocks_of(parts):
    found = []
    for i, (a, lanes, half, others) in enumerate(parts):
        for lane in range(0, lanes, 512):
            size = min(512, lanes - lane)
            fixed = a + lane + (half if others else 0)
            found.append((i, lane, size, (fixed, -half if others else half)))
    return found


def output_kernel(parts, side_ref, *refs):
    hidden, down, arrived = refs[:4], refs[4:6], refs[6 : 6 + 2 * len(parts)]
    out, result, sems = refs[-3:]
    side = side_ref[0]
    stores, at = [], 0
    for n, (i, lane, size, (fixed, turn)) in enumerate(blocks_of(parts)):
        column = pl.ds(pl.multiple_of(fixed + side * turn, 128), size)
        spot = pl.ds(at, size)
        at += size
        total = None
        for m in range(4):
            if m < 2:
                weight = down[m][:, column]
            else:
                weight = arrived[2 * i + m - 2][:, lane : lane + size]
            term = jnp.dot(hidden[m][...], weight, preferred_element_type=jnp.float32)
            total = term if total is None else total + term
        result[:, spot] = total.astype(result.dtype)
        stores.append(
            pltpu.make_async_copy(result.at[:, spot], out.at[:, column], sems.at[n])
        )
        stores[-1].start()
    for copy in stores:
        copy.wait()


def output_part(result, parts, side, hidden, down, arrived):
    rows, width = hidden[0].shape[0], down[0].shape[1]
    lanes = sum(part[1] for part in parts)
    operands = [side, *hidden, *down, *arrived]
    in_specs = (
        [pl.BlockSpec(memory_space=pltpu.SMEM)]
        + [pl.BlockSpec(memory_space=pltpu.VMEM)] * (6 + len(arrived))
    )
    aliases = {}
    if result is not None:
        aliases = {len(operands): 0}
        operands.append(result)
        in_specs.append(ANY)
    return call(
        functools.partial(output_kernel, parts),
        operands,
        in_specs,
        jax.ShapeDtypeStruct((rows, width), jnp.bfloat16),
        ANY,
        [
            pltpu.VMEM((rows, lanes), jnp.bfloat16),
            pltpu.SemaphoreType.DMA((len(blocks_of(parts)),)),
        ],
        aliases,
    )


def over_slices(partial_value):
    return [
        shifted(partial_value, "tensor", distance)
        for distance in range(1, lax.axis_size("tensor"))
    ]


def on_device(tokens, gate_weight, up_weight, down_weight):
    units, width = gate_weight.shape
    group = lax.axis_index("groups").astype(jnp.int32)
    first = group == 0
    side = group.reshape(1)

    spans = cuts(width, 128, FEATURE_SHARES)
    lane_cuts = [(2 * a, 2 * b) for a, b in cuts(width // 2, 128, LANE_SHARES)]
    count = len(spans)
    total_count = count + len(lane_cuts)
    relayed = total_count - WHOLES

    def piece(i, *after):
        if i < count:
            a, b = spans[i]
            gate, up = gate_weight, up_weight
            if after:
                gate, up = lax.optimization_barrier((gate, up, *after))[:2]
            return jnp.where(first, gate[:, a:b], up[:, a:b])
        a, b = lane_cuts[i - count]
        mid = (a + b) // 2
        down = tied(down_weight, *after)
        if i >= relayed:
            return down[:, a:b]
        return jnp.where(first, down[:, a:mid], down[:, mid:b])

    pieces = [piece(0)]
    pieces.append(piece(1, pieces[0]))
    pieces += [piece(i, pieces[1]) for i in range(2, total_count)]
    waiting = [shifted(pieces[i], "dp", 1) for i in range(QUEUE)]
    landed, crossed, mates, crossed_mates = [], {}, {}, {}

    def advance(*after):
        i = len(landed)
        held = [*after, *landed[-1:]]
        held += [crossed[j] for j in range(count) if j + SWAP_WAIT == i]
        block = tied(waiting[i], *held)
        landed.append(block)
        if i < relayed:
            crossed[i] = across(block)
        if i + QUEUE < total_count:
            waiting.append(shifted(tied(pieces[i + QUEUE], block), "dp", 1))
        return block

    def pass_own(n, *after):
        mates[count + n] = mate(tied(landed[count + n], *after))

    def pass_other(n, *after):
        crossed_mates[count + n] = mate(tied(crossed[count + n], *after))

    def batch(lo, hi, now, before=None):
        held = [block for i in range(lo, hi) for block in (landed[i], crossed[i])]
        held = lax.optimization_barrier((*held, now))[:-1]
        kind = jnp.bfloat16 if hi == count else jnp.float32
        return products([tokens, tokens_mate], held, spans[lo:hi], before, kind)

    tokens_mate = mate(tied(tokens, pieces[0]))
    down_mate = mate(tied(down_weight, pieces[1]))
    due = {0: pieces[2:], OWN: [tokens_mate, down_mate]}
    value = own_value = None
    for i in range(relayed):
        now = advance(*due.get(i, []))
        after = due.setdefault(i + 1, [])
        if i == OWN:
            own_value = products(
                [tied(tokens, now), tokens_mate], [gate_weight, up_weight], [(0, width)]
            )
            own_sent = over_slices(own_value)
            after.append(own_value)
        if i == OWN_SUM:
            here, given = activated(
                side, own_value, [tied(block, now) for block in own_sent], False
            )
            here_mate = mate(given)
            after.append(here)
            due.setdefault(OWN_MATE, []).append(here_mate)
        for stage, lo, hi in BATCHES:
            if i == stage:
                value = batch(lo, hi, now, value)
                after.append(value)
                if hi == count:
                    sent = over_slices(value)
        if i == PASS[0]:
            pass_own(0, now)
        if i == PASS[1]:
            pass_other(0, now)
    there, given = activated(side, value, [tied(block, now) for block in sent], True)
    there_mate = mate(given)
    if HOLD:
        there_mate = tied(there_mate, crossed[count + 1])

    def write(result, *which):
        parts, arrived = [], []
        for mark in which:
            n = mark if mark >= 0 else -1 - mark
            i = count + n
            a, b = lane_cuts[n]
            half = (b - a) // 2
            if i >= relayed:
                parts.append((a, b - a, 0, False))
                arrived += [landed[i], mates[i]]
            elif mark < 0:
                parts.append((a, half, half, True))
                arrived += [crossed[i], crossed_mates[i]]
            else:
                parts.append((a, half, half, False))
                arrived += [landed[i], mates[i]]
        return output_part(
            result,
            tuple(parts),
            side,
            [here, here_mate, there, there_mate],
            [down_weight, down_mate],
            arrived,
        )

    result = None
    for step in TAIL:
        kind, numbers = step[0], step[1:]
        if kind == "own":
            for n in numbers:
                pass_own(n, now, *([] if result is None else [result]))
        elif kind == "other":
            for n in numbers:
                pass_other(n, now, *([] if result is None else [result]))
        elif kind == "write":
            result = write(result, *numbers)
        elif kind == "last":
            held = [] if result is None else [result]
            held += [crossed[count + n] for n in numbers]
            now = advance(*held)
            pass_own(len(landed) - 1 - count, now)
    return result


def solution(mesh):
    return jax.shard_map(
        on_device,
        mesh=mesh,
        in_specs=(
            P(("groups", "dp", "sub"), "tensor"),
            P(("dp", "sub"), "tensor"),
            P(("dp", "sub"), "tensor"),
            P(("dp", "sub"), "tensor"),
        ),
        out_specs=P(("groups", "dp", "sub"), "tensor"),
        check_vma=False,
    )
```

```python
import functools

import jax
import jax.numpy as jnp
from jax import lax
from jax.experimental import pallas as pl
from jax.experimental.pallas import tpu as pltpu
from jax.sharding import PartitionSpec as P

FEATURE_SHARES = (1,) * 8
LANE_SHARES = (10, 13, 9)
WHOLES = 1
FIRST = 1
QUEUE = 2
OWN, OWN_SUM, OWN_MATE = 1, 4, 6
BATCHES = ((5, 0, 4), (7, 4, 7), (8, 7, 8))
PASS = (8, 9)
TAIL = (("own", 1), ("write", 0, -1, 1), ("ready", 2, -2), ("other", 1), ("last", 1), ("write", 2), ("write", -2))
SWAP_WAIT = 2
HOLD = 0
VMEM = 16 * 1024 * 1024
ANY = pl.BlockSpec(memory_space=pl.ANY)


def shifted(block, axis, distance):
    devices = range(lax.axis_size(axis))
    route = [((i - distance) % len(devices), i) for i in devices]
    return lax.ppermute(block, axis, route)


def mate(block):
    return shifted(block, "sub", 1)


def across(block):
    return shifted(block, "groups", 1)


def tied(value, *earlier):
    return lax.optimization_barrier((value, *earlier))[0] if earlier else value


def cuts(total, unit, shares):
    units, whole, done, marks = total // unit, sum(shares), 0, [0]
    for share in shares:
        done += share
        marks.append(units * done // whole * unit)
    marks[-1] = total
    return list(zip(marks[:-1], marks[1:]))


def call(kernel, operands, in_specs, out, out_spec, scratch, aliases):
    return pl.pallas_call(
        kernel,
        in_specs=in_specs,
        out_specs=out_spec,
        out_shape=out,
        scratch_shapes=scratch,
        input_output_aliases=aliases,
        compiler_params=pltpu.CompilerParams(vmem_limit_bytes=VMEM),
        cost_estimate=pl.CostEstimate(flops=1, bytes_accessed=1, transcendentals=0),
    )(*operands)


def products_kernel(sets, groups, spans, before, *refs):
    row_refs, unit_refs = refs[:sets], refs[sets : sets + groups * len(spans)]
    out, total = refs[-2:]
    for step, (a, b) in enumerate(spans):
        units = jnp.concatenate(
            [ref[:, : b - a] for ref in unit_refs[step * groups : (step + 1) * groups]], axis=0
        )
        rows = jnp.concatenate([ref[:, a:b] for ref in row_refs], axis=0)
        value = lax.dot_general(
            units, rows, (((1,), (1,)), ((), ())), preferred_element_type=jnp.float32
        )
        if step > 0:
            value += total[...]
        elif before:
            value += refs[-3][...]
        if step < len(spans) - 1:
            total[...] = value
        else:
            out[...] = value.astype(out.dtype)


WHOLE = pl.BlockSpec(memory_space=pltpu.VMEM)


def products(row_sets, unit_sets, spans, before=None, out_type=jnp.bfloat16):
    groups = len(unit_sets) // len(spans)
    shape = (sum(u.shape[0] for u in unit_sets[:groups]), sum(r.shape[0] for r in row_sets))
    operands = (*row_sets, *unit_sets)
    if before is not None:
        operands += (before,)
    return call(
        functools.partial(
            products_kernel, len(row_sets), groups, tuple(spans), before is not None
        ),
        operands,
        [WHOLE] * len(operands),
        jax.ShapeDtypeStruct(shape, out_type),
        WHOLE,
        [pltpu.VMEM(shape, jnp.float32)],
        {},
    )


def activation_kernel(turned, side_ref, *refs):
    terms, outs = refs[:-2], refs[-2:]
    rows, units = outs[0].shape
    total = terms[0][...].astype(jnp.float32)
    for ref in terms[1:]:
        total += ref[...].astype(jnp.float32)
    gate, up = total[:units], total[units:]
    if turned:
        first = side_ref[0] == 0
        gate, up = jnp.where(first, gate, up), jnp.where(first, up, gate)
    hidden = (gate / (1.0 + jnp.exp(-gate)) * up).T
    for i, out in enumerate(outs):
        out[...] = hidden[i * rows : (i + 1) * rows].astype(out.dtype)


def activated(side, value, others, turned):
    operands = [side, value, *others]
    shape = (value.shape[1] // 2, value.shape[0] // 2)
    return call(
        functools.partial(activation_kernel, turned),
        operands,
        [pl.BlockSpec(memory_space=pltpu.SMEM)] + [WHOLE] * (len(operands) - 1),
        [jax.ShapeDtypeStruct(shape, jnp.bfloat16)] * 2,
        [WHOLE] * 2,
        [],
        {},
    )


def blocks_of(parts):
    found = []
    for i, (a, lanes, half, others) in enumerate(parts):
        for lane in range(0, lanes, 512):
            size = min(512, lanes - lane)
            fixed = a + lane + (half if others else 0)
            found.append((i, lane, size, (fixed, -half if others else half)))
    return found


def columns_of(side_ref, parts):
    side, at = side_ref[0], 0
    for i, lane, size, (fixed, turn) in blocks_of(parts):
        column = pl.ds(pl.multiple_of(fixed + side * turn, 128), size)
        yield pl.ds(at, size), i, slice(lane, lane + size), column
        at += size


def terms_sum(total, terms):
    for rows, weight in terms:
        term = jnp.dot(rows[...], weight, preferred_element_type=jnp.float32)
        total = term if total is None else total + term
    return total


def own_part_kernel(parts, side_ref, *refs):
    hidden, down, outs = refs[:2], refs[2:4], refs[4:]
    for _, i, lanes, column in columns_of(side_ref, parts):
        outs[i][:, lanes] = terms_sum(
            None, [(rows, ref[:, column]) for rows, ref in zip(hidden, down)]
        )


def own_parts(parts, side, hidden, down):
    return call(
        functools.partial(own_part_kernel, parts),
        [side, *hidden, *down],
        [pl.BlockSpec(memory_space=pltpu.SMEM)] + [WHOLE] * 4,
        [jax.ShapeDtypeStruct((hidden[0].shape[0], part[1]), jnp.float32) for part in parts],
        [WHOLE] * len(parts),
        [],
        {},
    )


def output_kernel(parts, known, side_ref, *refs):
    near = 1 if known else 4
    arrived = refs[2 : 2 + 2 * len(parts)]
    given = refs[2 + 2 * len(parts) : 2 + 2 * len(parts) + near]
    out, result, sems = refs[-3:]
    stores = []
    for n, (spot, i, lanes, column) in enumerate(columns_of(side_ref, parts)):
        terms = [(refs[m], arrived[2 * i + m][:, lanes]) for m in range(2)]
        if known:
            total = terms_sum(given[0][:, lanes], terms)
        else:
            total = terms_sum(None, [(given[m], given[2 + m][:, column]) for m in range(2)] + terms)
        result[:, spot] = total.astype(result.dtype)
        stores.append(
            pltpu.make_async_copy(result.at[:, spot], out.at[:, column], sems.at[n])
        )
        stores[-1].start()
    for copy in stores:
        copy.wait()


def output_part(result, parts, side, there, arrived, given, width):
    rows = there[0].shape[0]
    lanes = sum(part[1] for part in parts)
    operands = [side, *there, *arrived, *given]
    in_specs = [pl.BlockSpec(memory_space=pltpu.SMEM)] + [WHOLE] * (len(operands) - 1)
    aliases = {}
    if result is not None:
        aliases = {len(operands): 0}
        operands.append(result)
        in_specs.append(ANY)
    return call(
        functools.partial(output_kernel, parts, len(given) == 1),
        operands,
        in_specs,
        jax.ShapeDtypeStruct((rows, width), jnp.bfloat16),
        ANY,
        [
            pltpu.VMEM((rows, lanes), jnp.bfloat16),
            pltpu.SemaphoreType.DMA((len(blocks_of(parts)),)),
        ],
        aliases,
    )


def over_slices(partial_value):
    return [
        shifted(partial_value, "tensor", distance)
        for distance in range(1, lax.axis_size("tensor"))
    ]


def on_device(tokens, gate_weight, up_weight, down_weight):
    units, width = gate_weight.shape
    group = lax.axis_index("groups").astype(jnp.int32)
    first = group == 0
    side = group.reshape(1)

    spans = cuts(width, 128, FEATURE_SHARES)
    lane_cuts = [(2 * a, 2 * b) for a, b in cuts(width // 2, 128, LANE_SHARES)]
    count = len(spans)
    total_count = count + len(lane_cuts)
    relayed = total_count - WHOLES

    def piece(i, *after):
        if i < count:
            a, b = spans[i]
            gate, up = gate_weight, up_weight
            if after:
                gate, up = lax.optimization_barrier((gate, up, *after))[:2]
            return jnp.where(first, gate[:, a:b], up[:, a:b])
        a, b = lane_cuts[i - count]
        mid = (a + b) // 2
        down = tied(down_weight, *after)
        if i >= relayed:
            return down[:, a:b]
        return jnp.where(first, down[:, a:mid], down[:, mid:b])

    pieces = [piece(0)]
    pieces.append(piece(1, pieces[0]))
    pieces += [piece(i, pieces[FIRST]) for i in range(2, total_count)]
    waiting = [shifted(pieces[i], "dp", 1) for i in range(QUEUE)]
    landed, crossed, mates, crossed_mates = [], {}, {}, {}

    def advance(*after):
        i = len(landed)
        held = [*after, *landed[-1:]]
        held += [crossed[j] for j in range(count) if j + SWAP_WAIT == i]
        block = tied(waiting[i], *held)
        landed.append(block)
        if i < relayed:
            crossed[i] = across(block)
        if i + QUEUE < total_count:
            waiting.append(shifted(tied(pieces[i + QUEUE], block), "dp", 1))
        return block

    def pass_own(n, *after):
        mates[count + n] = mate(tied(landed[count + n], *after))

    def pass_other(n, *after):
        crossed_mates[count + n] = mate(tied(crossed[count + n], *after))

    def batch(lo, hi, now, before=None):
        held = [block for i in range(lo, hi) for block in (landed[i], crossed[i])]
        held = lax.optimization_barrier((*held, now))[:-1]
        kind = jnp.bfloat16 if hi == count else jnp.float32
        return products([tokens, tokens_mate], held, spans[lo:hi], before, kind)

    tokens_mate = mate(tied(tokens, pieces[0]))
    down_mate = mate(tied(down_weight, pieces[1]))
    due = {0: pieces[2:], OWN: [tokens_mate, down_mate]}
    value = own_value = None
    for i in range(relayed):
        now = advance(*due.get(i, []))
        after = due.setdefault(i + 1, [])
        if i == OWN:
            own_value = products(
                [tied(tokens, now), tokens_mate], [gate_weight, up_weight], [(0, width)]
            )
            own_sent = over_slices(own_value)
            after.append(own_value)
        if i == OWN_SUM:
            here, given = activated(
                side, own_value, [tied(block, now) for block in own_sent], False
            )
            here_mate = mate(given)
            after.append(here)
            due.setdefault(OWN_MATE, []).append(here_mate)
        for stage, lo, hi in BATCHES:
            if i == stage:
                value = batch(lo, hi, now, value)
                after.append(value)
                if hi == count:
                    sent = over_slices(value)
        if i == PASS[0]:
            pass_own(0, now)
        if i == PASS[1]:
            pass_other(0, now)
    there, given = activated(side, value, [tied(block, now) for block in sent], True)
    there_mate = mate(given)
    if HOLD:
        there_mate = tied(there_mate, crossed[count + 1])

    ready = {}

    def part_of(mark):
        n = mark if mark >= 0 else -1 - mark
        a, b = lane_cuts[n]
        half = (b - a) // 2
        if count + n >= relayed:
            return a, b - a, 0, False
        return a, half, half, mark < 0

    def write(result, *which):
        arrived = []
        for mark in which:
            if mark < 0:
                arrived += [crossed[count - 1 - mark], crossed_mates[count - 1 - mark]]
            else:
                arrived += [landed[count + mark], mates[count + mark]]
        given = [here, here_mate, down_weight, down_mate]
        if which[0] in ready:
            given = [ready[which[0]]]
        return output_part(
            result,
            tuple(part_of(mark) for mark in which),
            side,
            [there, there_mate],
            arrived,
            given,
            width,
        )

    result = None
    for step in TAIL:
        kind, numbers = step[0], step[1:]
        if kind == "own":
            for n in numbers:
                pass_own(n, now, *([] if result is None else [result]))
        elif kind == "other":
            for n in numbers:
                pass_other(n, now, *([] if result is None else [result]))
        elif kind == "write":
            result = write(result, *numbers)
        elif kind == "ready":
            found = own_parts(
                tuple(part_of(mark) for mark in numbers),
                side,
                [here, tied(here_mate, result)],
                [down_weight, down_mate],
            )
            ready.update(zip(numbers, found))
        elif kind == "last":
            held = [] if result is None else [result]
            held += ready.values()
            held += [crossed[count + n] for n in numbers]
            now = advance(*held)
            pass_own(len(landed) - 1 - count, now)
    return result


def solution(mesh):
    return jax.shard_map(
        on_device,
        mesh=mesh,
        in_specs=(
            P(("groups", "dp", "sub"), "tensor"),
            P(("dp", "sub"), "tensor"),
            P(("dp", "sub"), "tensor"),
            P(("dp", "sub"), "tensor"),
        ),
        out_specs=P(("groups", "dp", "sub"), "tensor"),
        check_vma=False,
    )
```

```python
import functools

import jax
import jax.numpy as jnp
from jax import lax
from jax.experimental import pallas as pl
from jax.experimental.pallas import tpu as pltpu
from jax.sharding import PartitionSpec as P

FEATURE_SHARES = (1,) * 8
LANE_SHARES = (10, 13, 9)
WHOLES = 1
QUEUE = 2
OWN, OWN_SUM, OWN_MATE = 1, 4, 6
BATCHES = ((5, 0, 4), (7, 4, 7), (8, 7, 8))
PASS = (8, 9)
TAIL = (("own", 1), ("write", 0, -1, 1), ("ready", 2, -2), ("other", 1), ("last", 1), ("write", 2), ("write", -2))
SWAP_WAIT = 2
VMEM = 16 * 1024 * 1024
ANY = pl.BlockSpec(memory_space=pl.ANY)


def shifted(block, axis, distance):
    devices = range(lax.axis_size(axis))
    route = [((i - distance) % len(devices), i) for i in devices]
    return lax.ppermute(block, axis, route)


def mate(block):
    return shifted(block, "sub", 1)


def across(block):
    return shifted(block, "groups", 1)


def tied(value, *earlier):
    return lax.optimization_barrier((value, *earlier))[0] if earlier else value


def cuts(total, unit, shares):
    units, whole, done, marks = total // unit, sum(shares), 0, [0]
    for share in shares:
        done += share
        marks.append(units * done // whole * unit)
    marks[-1] = total
    return list(zip(marks[:-1], marks[1:]))


def call(kernel, operands, in_specs, out, out_spec, scratch, aliases):
    return pl.pallas_call(
        kernel,
        in_specs=in_specs,
        out_specs=out_spec,
        out_shape=out,
        scratch_shapes=scratch,
        input_output_aliases=aliases,
        compiler_params=pltpu.CompilerParams(vmem_limit_bytes=VMEM),
        cost_estimate=pl.CostEstimate(flops=1, bytes_accessed=1, transcendentals=0),
    )(*operands)


def products_kernel(sets, groups, spans, before, *refs):
    row_refs, unit_refs = refs[:sets], refs[sets : sets + groups * len(spans)]
    out, total = refs[-2:]
    for step, (a, b) in enumerate(spans):
        units = jnp.concatenate(
            [ref[:, : b - a] for ref in unit_refs[step * groups : (step + 1) * groups]], axis=0
        )
        rows = jnp.concatenate([ref[:, a:b] for ref in row_refs], axis=0)
        value = lax.dot_general(
            units, rows, (((1,), (1,)), ((), ())), preferred_element_type=jnp.float32
        )
        if step > 0:
            value += total[...]
        elif before:
            value += refs[-3][...]
        if step < len(spans) - 1:
            total[...] = value
        else:
            out[...] = value.astype(out.dtype)


WHOLE = pl.BlockSpec(memory_space=pltpu.VMEM)


def products(row_sets, unit_sets, spans, before=None, out_type=jnp.bfloat16):
    groups = len(unit_sets) // len(spans)
    shape = (sum(u.shape[0] for u in unit_sets[:groups]), sum(r.shape[0] for r in row_sets))
    operands = (*row_sets, *unit_sets)
    if before is not None:
        operands += (before,)
    return call(
        functools.partial(
            products_kernel, len(row_sets), groups, tuple(spans), before is not None
        ),
        operands,
        [WHOLE] * len(operands),
        jax.ShapeDtypeStruct(shape, out_type),
        WHOLE,
        [pltpu.VMEM(shape, jnp.float32)],
        {},
    )


def activation_kernel(turned, side_ref, *refs):
    terms, outs = refs[:-2], refs[-2:]
    rows, units = outs[0].shape
    total = terms[0][...].astype(jnp.float32)
    for ref in terms[1:]:
        total += ref[...].astype(jnp.float32)
    gate, up = total[:units], total[units:]
    if turned:
        first = side_ref[0] == 0
        gate, up = jnp.where(first, gate, up), jnp.where(first, up, gate)
    hidden = (gate / (1.0 + jnp.exp(-gate)) * up).T
    for i, out in enumerate(outs):
        out[...] = hidden[i * rows : (i + 1) * rows].astype(out.dtype)


def activated(side, value, others, turned):
    operands = [side, value, *others]
    shape = (value.shape[1] // 2, value.shape[0] // 2)
    return call(
        functools.partial(activation_kernel, turned),
        operands,
        [pl.BlockSpec(memory_space=pltpu.SMEM)] + [WHOLE] * (len(operands) - 1),
        [jax.ShapeDtypeStruct(shape, jnp.bfloat16)] * 2,
        [WHOLE] * 2,
        [],
        {},
    )


def blocks_of(parts):
    found = []
    for i, (a, lanes, half, others) in enumerate(parts):
        for lane in range(0, lanes, 512):
            size = min(512, lanes - lane)
            fixed = a + lane + (half if others else 0)
            found.append((i, lane, size, (fixed, -half if others else half)))
    return found


def columns_of(side_ref, parts):
    side, at = side_ref[0], 0
    for i, lane, size, (fixed, turn) in blocks_of(parts):
        column = pl.ds(pl.multiple_of(fixed + side * turn, 128), size)
        yield pl.ds(at, size), i, slice(lane, lane + size), column
        at += size


def terms_sum(total, terms):
    for rows, weight in terms:
        term = jnp.dot(rows[...], weight, preferred_element_type=jnp.float32)
        total = term if total is None else total + term
    return total


def own_part_kernel(parts, side_ref, *refs):
    hidden, down, outs = refs[:2], refs[2:4], refs[4:]
    for _, i, lanes, column in columns_of(side_ref, parts):
        outs[i][:, lanes] = terms_sum(
            None, [(rows, ref[:, column]) for rows, ref in zip(hidden, down)]
        )


def own_parts(parts, side, hidden, down):
    return call(
        functools.partial(own_part_kernel, parts),
        [side, *hidden, *down],
        [pl.BlockSpec(memory_space=pltpu.SMEM)] + [WHOLE] * 4,
        [jax.ShapeDtypeStruct((hidden[0].shape[0], part[1]), jnp.float32) for part in parts],
        [WHOLE] * len(parts),
        [],
        {},
    )


def output_kernel(parts, known, side_ref, *refs):
    near = 1 if known else 4
    arrived = refs[2 : 2 + 2 * len(parts)]
    given = refs[2 + 2 * len(parts) : 2 + 2 * len(parts) + near]
    out, result, sems = refs[-3:]
    stores = []
    for n, (spot, i, lanes, column) in enumerate(columns_of(side_ref, parts)):
        terms = [(refs[m], arrived[2 * i + m][:, lanes]) for m in range(2)]
        if known:
            total = terms_sum(given[0][:, lanes], terms)
        else:
            total = terms_sum(None, [(given[m], given[2 + m][:, column]) for m in range(2)] + terms)
        result[:, spot] = total.astype(result.dtype)
        stores.append(
            pltpu.make_async_copy(result.at[:, spot], out.at[:, column], sems.at[n])
        )
        stores[-1].start()
    for copy in stores:
        copy.wait()


def output_part(result, parts, side, there, arrived, given, width):
    rows = there[0].shape[0]
    lanes = sum(part[1] for part in parts)
    operands = [side, *there, *arrived, *given]
    in_specs = [pl.BlockSpec(memory_space=pltpu.SMEM)] + [WHOLE] * (len(operands) - 1)
    aliases = {}
    if result is not None:
        aliases = {len(operands): 0}
        operands.append(result)
        in_specs.append(ANY)
    return call(
        functools.partial(output_kernel, parts, len(given) == 1),
        operands,
        in_specs,
        jax.ShapeDtypeStruct((rows, width), jnp.bfloat16),
        ANY,
        [
            pltpu.VMEM((rows, lanes), jnp.bfloat16),
            pltpu.SemaphoreType.DMA((len(blocks_of(parts)),)),
        ],
        aliases,
    )


def over_slices(partial_value):
    return [
        shifted(partial_value, "tensor", distance)
        for distance in range(1, lax.axis_size("tensor"))
    ]


def on_device(tokens, gate_weight, up_weight, down_weight):
    units, width = gate_weight.shape
    group = lax.axis_index("groups").astype(jnp.int32)
    first = group == 0
    side = group.reshape(1)

    spans = cuts(width, 128, FEATURE_SHARES)
    lane_cuts = [(2 * a, 2 * b) for a, b in cuts(width // 2, 128, LANE_SHARES)]
    count = len(spans)
    total_count = count + len(lane_cuts)
    relayed = total_count - WHOLES

    def piece(i, *after):
        if i < count:
            a, b = spans[i]
            gate, up = gate_weight, up_weight
            if after:
                gate, up = lax.optimization_barrier((gate, up, *after))[:2]
            return jnp.where(first, gate[:, a:b], up[:, a:b])
        a, b = lane_cuts[i - count]
        mid = (a + b) // 2
        down = tied(down_weight, *after)
        if i >= relayed:
            return down[:, a:b]
        return jnp.where(first, down[:, a:mid], down[:, mid:b])

    pieces = [piece(0), piece(1)]
    pieces += [piece(i, pieces[1]) for i in range(2, total_count)]
    waiting = [shifted(pieces[i], "dp", 1) for i in range(QUEUE)]
    landed, crossed, mates, crossed_mates = [], {}, {}, {}

    def advance(*after):
        i = len(landed)
        held = [*after, *landed[-1:]]
        held += [crossed[j] for j in range(count) if j + SWAP_WAIT == i]
        block = tied(waiting[i], *held)
        landed.append(block)
        if i < relayed:
            crossed[i] = across(block)
        if i + QUEUE < total_count:
            waiting.append(shifted(tied(pieces[i + QUEUE], block), "dp", 1))
        return block

    def pass_own(n, *after):
        mates[count + n] = mate(tied(landed[count + n], *after))

    def pass_other(n, *after):
        crossed_mates[count + n] = mate(tied(crossed[count + n], *after))

    def batch(lo, hi, now, before=None):
        held = [block for i in range(lo, hi) for block in (landed[i], crossed[i])]
        held = lax.optimization_barrier((*held, now))[:-1]
        kind = jnp.bfloat16 if hi == count else jnp.float32
        return products([tokens, tokens_mate], held, spans[lo:hi], before, kind)

    tokens_mate = mate(tied(tokens, pieces[0]))
    down_mate = mate(tied(down_weight, pieces[1]))
    due = {0: pieces[2:], OWN: [tokens_mate, down_mate]}
    value = own_value = None
    for i in range(relayed):
        now = advance(*due.get(i, []))
        after = due.setdefault(i + 1, [])
        if i == OWN:
            own_value = products(
                [tied(tokens, now), tokens_mate], [gate_weight, up_weight], [(0, width)]
            )
            own_sent = over_slices(own_value)
            after.append(own_value)
        if i == OWN_SUM:
            here, given = activated(
                side, own_value, [tied(block, now) for block in own_sent], False
            )
            here_mate = mate(given)
            after.append(here)
            due.setdefault(OWN_MATE, []).append(here_mate)
        for stage, lo, hi in BATCHES:
            if i == stage:
                value = batch(lo, hi, now, value)
                after.append(value)
                if hi == count:
                    sent = over_slices(value)
        if i == PASS[0]:
            pass_own(0, now)
        if i == PASS[1]:
            pass_other(0, now)
    there, given = activated(side, value, [tied(block, now) for block in sent], True)
    there_mate = mate(given)

    ready = {}

    def part_of(mark):
        n = mark if mark >= 0 else -1 - mark
        a, b = lane_cuts[n]
        half = (b - a) // 2
        if count + n >= relayed:
            return a, b - a, 0, False
        return a, half, half, mark < 0

    def write(result, *which):
        arrived = []
        for mark in which:
            if mark < 0:
                arrived += [crossed[count - 1 - mark], crossed_mates[count - 1 - mark]]
            else:
                arrived += [landed[count + mark], mates[count + mark]]
        given = [here, here_mate, down_weight, down_mate]
        if which[0] in ready:
            given = [ready[which[0]]]
        return output_part(
            result,
            tuple(part_of(mark) for mark in which),
            side,
            [there, there_mate],
            arrived,
            given,
            width,
        )

    result = None
    for step in TAIL:
        kind, numbers = step[0], step[1:]
        if kind == "own":
            for n in numbers:
                pass_own(n, now, *([] if result is None else [result]))
        elif kind == "other":
            for n in numbers:
                pass_other(n, now, *([] if result is None else [result]))
        elif kind == "write":
            result = write(result, *numbers)
        elif kind == "ready":
            found = own_parts(
                tuple(part_of(mark) for mark in numbers),
                side,
                [here, tied(here_mate, result)],
                [down_weight, down_mate],
            )
            ready.update(zip(numbers, found))
        elif kind == "last":
            held = [] if result is None else [result]
            held += ready.values()
            held += [crossed[count + n] for n in numbers]
            now = advance(*held)
            pass_own(len(landed) - 1 - count, now)
    return result


def solution(mesh):
    return jax.shard_map(
        on_device,
        mesh=mesh,
        in_specs=(
            P(("groups", "dp", "sub"), "tensor"),
            P(("dp", "sub"), "tensor"),
            P(("dp", "sub"), "tensor"),
            P(("dp", "sub"), "tensor"),
        ),
        out_specs=P(("groups", "dp", "sub"), "tensor"),
        check_vma=False,
    )
```

```python
import functools

import jax
import jax.numpy as jnp
from jax import lax
from jax.experimental import pallas as pl
from jax.experimental.pallas import tpu as pltpu
from jax.sharding import PartitionSpec as P

FEATURE_SHARES = (1,) * 8
LANE_SHARES = (10, 14, 8)
WHOLES = 1
QUEUE = 2
OWN, OWN_SUM, OWN_MATE = 1, 4, 6
BATCHES = ((5, 0, 4), (7, 4, 7), (8, 7, 8))
PASS = (8, 9)
TAIL = (("own", 1), ("write", 0, -1, 1), ("ready", 2, -2), ("other", 1), ("last",), ("write", 2), ("write", -2))
SWAP_WAIT = 2
VMEM = 16 * 1024 * 1024
ANY = pl.BlockSpec(memory_space=pl.ANY)


def shifted(block, axis, distance):
    devices = range(lax.axis_size(axis))
    route = [((i - distance) % len(devices), i) for i in devices]
    return lax.ppermute(block, axis, route)


def mate(block):
    return shifted(block, "sub", 1)


def across(block):
    return shifted(block, "groups", 1)


def tied(value, *earlier):
    return lax.optimization_barrier((value, *earlier))[0] if earlier else value


def cuts(total, unit, shares):
    units, whole, done, marks = total // unit, sum(shares), 0, [0]
    for share in shares:
        done += share
        marks.append(units * done // whole * unit)
    marks[-1] = total
    return list(zip(marks[:-1], marks[1:]))


def call(kernel, operands, in_specs, out, out_spec, scratch, aliases):
    return pl.pallas_call(
        kernel,
        in_specs=in_specs,
        out_specs=out_spec,
        out_shape=out,
        scratch_shapes=scratch,
        input_output_aliases=aliases,
        compiler_params=pltpu.CompilerParams(vmem_limit_bytes=VMEM),
        cost_estimate=pl.CostEstimate(flops=1, bytes_accessed=1, transcendentals=0),
    )(*operands)


def products_kernel(sets, groups, spans, before, *refs):
    row_refs, unit_refs = refs[:sets], refs[sets : sets + groups * len(spans)]
    out, total = refs[-2:]
    for step, (a, b) in enumerate(spans):
        units = jnp.concatenate(
            [ref[:, : b - a] for ref in unit_refs[step * groups : (step + 1) * groups]], axis=0
        )
        rows = jnp.concatenate([ref[:, a:b] for ref in row_refs], axis=0)
        value = lax.dot_general(
            units, rows, (((1,), (1,)), ((), ())), preferred_element_type=jnp.float32
        )
        if step > 0:
            value += total[...]
        elif before:
            value += refs[-3][...]
        if step < len(spans) - 1:
            total[...] = value
        else:
            out[...] = value.astype(out.dtype)


WHOLE = pl.BlockSpec(memory_space=pltpu.VMEM)


def products(row_sets, unit_sets, spans, before=None, out_type=jnp.bfloat16):
    groups = len(unit_sets) // len(spans)
    shape = (sum(u.shape[0] for u in unit_sets[:groups]), sum(r.shape[0] for r in row_sets))
    operands = (*row_sets, *unit_sets)
    if before is not None:
        operands += (before,)
    return call(
        functools.partial(
            products_kernel, len(row_sets), groups, tuple(spans), before is not None
        ),
        operands,
        [WHOLE] * len(operands),
        jax.ShapeDtypeStruct(shape, out_type),
        WHOLE,
        [pltpu.VMEM(shape, jnp.float32)],
        {},
    )


def activation_kernel(turned, side_ref, *refs):
    terms, outs = refs[:-2], refs[-2:]
    rows, units = outs[0].shape
    total = terms[0][...].astype(jnp.float32)
    for ref in terms[1:]:
        total += ref[...].astype(jnp.float32)
    gate, up = total[:units], total[units:]
    if turned:
        first = side_ref[0] == 0
        gate, up = jnp.where(first, gate, up), jnp.where(first, up, gate)
    hidden = (gate / (1.0 + jnp.exp(-gate)) * up).T
    for i, out in enumerate(outs):
        out[...] = hidden[i * rows : (i + 1) * rows].astype(out.dtype)


def activated(side, value, others, turned):
    operands = [side, value, *others]
    shape = (value.shape[1] // 2, value.shape[0] // 2)
    return call(
        functools.partial(activation_kernel, turned),
        operands,
        [pl.BlockSpec(memory_space=pltpu.SMEM)] + [WHOLE] * (len(operands) - 1),
        [jax.ShapeDtypeStruct(shape, jnp.bfloat16)] * 2,
        [WHOLE] * 2,
        [],
        {},
    )


def blocks_of(parts):
    found = []
    for i, (a, lanes, half, others) in enumerate(parts):
        for lane in range(0, lanes, 512):
            size = min(512, lanes - lane)
            fixed = a + lane + (half if others else 0)
            found.append((i, lane, size, (fixed, -half if others else half)))
    return found


def columns_of(side_ref, parts):
    side, at = side_ref[0], 0
    for i, lane, size, (fixed, turn) in blocks_of(parts):
        column = pl.ds(pl.multiple_of(fixed + side * turn, 128), size)
        yield pl.ds(at, size), i, slice(lane, lane + size), column
        at += size


def terms_sum(total, terms):
    for rows, weight in terms:
        term = jnp.dot(rows[...], weight, preferred_element_type=jnp.float32)
        total = term if total is None else total + term
    return total


def own_part_kernel(parts, side_ref, *refs):
    hidden, down, outs = refs[:2], refs[2:4], refs[4:]
    for _, i, lanes, column in columns_of(side_ref, parts):
        outs[i][:, lanes] = terms_sum(
            None, [(rows, ref[:, column]) for rows, ref in zip(hidden, down)]
        )


def own_parts(parts, side, hidden, down):
    return call(
        functools.partial(own_part_kernel, parts),
        [side, *hidden, *down],
        [pl.BlockSpec(memory_space=pltpu.SMEM)] + [WHOLE] * 4,
        [jax.ShapeDtypeStruct((hidden[0].shape[0], part[1]), jnp.float32) for part in parts],
        [WHOLE] * len(parts),
        [],
        {},
    )


def output_kernel(parts, known, side_ref, *refs):
    near = 1 if known else 4
    arrived = refs[2 : 2 + 2 * len(parts)]
    given = refs[2 + 2 * len(parts) : 2 + 2 * len(parts) + near]
    out, result, sems = refs[-3:]
    stores = []
    for n, (spot, i, lanes, column) in enumerate(columns_of(side_ref, parts)):
        terms = [(refs[m], arrived[2 * i + m][:, lanes]) for m in range(2)]
        if known:
            total = terms_sum(given[0][:, lanes], terms)
        else:
            total = terms_sum(None, [(given[m], given[2 + m][:, column]) for m in range(2)] + terms)
        result[:, spot] = total.astype(result.dtype)
        stores.append(
            pltpu.make_async_copy(result.at[:, spot], out.at[:, column], sems.at[n])
        )
        stores[-1].start()
    for copy in stores:
        copy.wait()


def output_part(result, parts, side, there, arrived, given, width):
    rows = there[0].shape[0]
    lanes = sum(part[1] for part in parts)
    operands = [side, *there, *arrived, *given]
    in_specs = [pl.BlockSpec(memory_space=pltpu.SMEM)] + [WHOLE] * (len(operands) - 1)
    aliases = {}
    if result is not None:
        aliases = {len(operands): 0}
        operands.append(result)
        in_specs.append(ANY)
    return call(
        functools.partial(output_kernel, parts, len(given) == 1),
        operands,
        in_specs,
        jax.ShapeDtypeStruct((rows, width), jnp.bfloat16),
        ANY,
        [
            pltpu.VMEM((rows, lanes), jnp.bfloat16),
            pltpu.SemaphoreType.DMA((len(blocks_of(parts)),)),
        ],
        aliases,
    )


def over_slices(partial_value):
    return [
        shifted(partial_value, "tensor", distance)
        for distance in range(1, lax.axis_size("tensor"))
    ]


def on_device(tokens, gate_weight, up_weight, down_weight):
    units, width = gate_weight.shape
    group = lax.axis_index("groups").astype(jnp.int32)
    first = group == 0
    side = group.reshape(1)

    spans = cuts(width, 128, FEATURE_SHARES)
    lane_cuts = [(2 * a, 2 * b) for a, b in cuts(width // 2, 128, LANE_SHARES)]
    count = len(spans)
    total_count = count + len(lane_cuts)
    relayed = total_count - WHOLES

    def piece(i, *after):
        if i < count:
            a, b = spans[i]
            gate, up = gate_weight, up_weight
            if after:
                gate, up = lax.optimization_barrier((gate, up, *after))[:2]
            return jnp.where(first, gate[:, a:b], up[:, a:b])
        a, b = lane_cuts[i - count]
        mid = (a + b) // 2
        down = tied(down_weight, *after)
        if i >= relayed:
            return down[:, a:b]
        return jnp.where(first, down[:, a:mid], down[:, mid:b])

    pieces = [piece(0), piece(1)]
    pieces += [piece(i, pieces[1]) for i in range(2, total_count)]
    waiting = [shifted(pieces[i], "dp", 1) for i in range(QUEUE)]
    landed, crossed, mates, crossed_mates = [], {}, {}, {}

    def advance(*after):
        i = len(landed)
        held = [*after, *landed[-1:]]
        held += [crossed[j] for j in range(count) if j + SWAP_WAIT == i]
        block = tied(waiting[i], *held)
        landed.append(block)
        if i < relayed:
            crossed[i] = across(block)
        if i + QUEUE < total_count:
            waiting.append(shifted(tied(pieces[i + QUEUE], block), "dp", 1))
        return block

    def pass_own(n, *after):
        mates[count + n] = mate(tied(landed[count + n], *after))

    def pass_other(n, *after):
        crossed_mates[count + n] = mate(tied(crossed[count + n], *after))

    def batch(lo, hi, now, before=None):
        held = [block for i in range(lo, hi) for block in (landed[i], crossed[i])]
        held = lax.optimization_barrier((*held, now))[:-1]
        kind = jnp.bfloat16 if hi == count else jnp.float32
        return products([tokens, tokens_mate], held, spans[lo:hi], before, kind)

    tokens_mate = mate(tied(tokens, pieces[0]))
    down_mate = mate(tied(down_weight, pieces[1]))
    due = {0: pieces[2:], OWN: [tokens_mate, down_mate]}
    value = own_value = None
    for i in range(relayed):
        now = advance(*due.get(i, []))
        after = due.setdefault(i + 1, [])
        if i == OWN:
            own_value = products(
                [tied(tokens, now), tokens_mate], [gate_weight, up_weight], [(0, width)]
            )
            own_sent = over_slices(own_value)
            after.append(own_value)
        if i == OWN_SUM:
            here, given = activated(
                side, own_value, [tied(block, now) for block in own_sent], False
            )
            here_mate = mate(given)
            after.append(here)
            due.setdefault(OWN_MATE, []).append(here_mate)
        for stage, lo, hi in BATCHES:
            if i == stage:
                value = batch(lo, hi, now, value)
                after.append(value)
                if hi == count:
                    sent = over_slices(value)
        if i == PASS[0]:
            pass_own(0, now)
        if i == PASS[1]:
            pass_other(0, now)
    there, given = activated(side, value, [tied(block, now) for block in sent], True)
    there_mate = mate(given)

    ready = {}

    def part_of(mark):
        n = mark if mark >= 0 else -1 - mark
        a, b = lane_cuts[n]
        half = (b - a) // 2
        if count + n >= relayed:
            return a, b - a, 0, False
        return a, half, half, mark < 0

    def write(result, *which):
        arrived = []
        for mark in which:
            if mark < 0:
                arrived += [crossed[count - 1 - mark], crossed_mates[count - 1 - mark]]
            else:
                arrived += [landed[count + mark], mates[count + mark]]
        given = [here, here_mate, down_weight, down_mate]
        if which[0] in ready:
            given = [ready[which[0]]]
        return output_part(
            result,
            tuple(part_of(mark) for mark in which),
            side,
            [there, there_mate],
            arrived,
            given,
            width,
        )

    result = None
    for step in TAIL:
        kind, numbers = step[0], step[1:]
        if kind == "own":
            for n in numbers:
                pass_own(n, now, *([] if result is None else [result]))
        elif kind == "other":
            for n in numbers:
                pass_other(n, now, *([] if result is None else [result]))
        elif kind == "write":
            result = write(result, *numbers)
        elif kind == "ready":
            found = own_parts(
                tuple(part_of(mark) for mark in numbers),
                side,
                [here, tied(here_mate, result)],
                [down_weight, down_mate],
            )
            ready.update(zip(numbers, found))
        elif kind == "last":
            held = [] if result is None else [result]
            held += ready.values()
            held += [crossed[count + n] for n in numbers]
            now = advance(*held)
            pass_own(len(landed) - 1 - count, now)
    return result


def solution(mesh):
    return jax.shard_map(
        on_device,
        mesh=mesh,
        in_specs=(
            P(("groups", "dp", "sub"), "tensor"),
            P(("dp", "sub"), "tensor"),
            P(("dp", "sub"), "tensor"),
            P(("dp", "sub"), "tensor"),
        ),
        out_specs=P(("groups", "dp", "sub"), "tensor"),
        check_vma=False,
    )
```

```python
import functools

import jax
import jax.numpy as jnp
from jax import lax
from jax.experimental import pallas as pl
from jax.experimental.pallas import tpu as pltpu
from jax.sharding import PartitionSpec as P

FEATURE_SHARES = (1,) * 8
LANE_SHARES = (10, 14, 8)
WHOLES = 1
QUEUE = 2
OWN, OWN_SUM, OWN_MATE = 1, 4, 6
BATCHES = ((5, 0, 4), (7, 4, 7), (8, 7, 8))
PASS = (8, 9)
TAIL = (("own", 1), ("write", 0, -1, 1), ("ready", 2, -2), ("other", 1), ("last",), ("write", 2), ("write", -2))
SWAP_WAIT = 2
VMEM = 16 * 1024 * 1024
ANY = pl.BlockSpec(memory_space=pl.ANY)


def shifted(block, axis, distance):
    devices = range(lax.axis_size(axis))
    route = [((i - distance) % len(devices), i) for i in devices]
    return lax.ppermute(block, axis, route)


def mate(block):
    return shifted(block, "sub", 1)


def across(block):
    return shifted(block, "groups", 1)


def tied(value, *earlier):
    return lax.optimization_barrier((value, *earlier))[0] if earlier else value


def cuts(total, unit, shares):
    units, whole, done, marks = total // unit, sum(shares), 0, [0]
    for share in shares:
        done += share
        marks.append(units * done // whole * unit)
    marks[-1] = total
    return list(zip(marks[:-1], marks[1:]))


def call(kernel, operands, in_specs, out, out_spec, scratch, aliases):
    return pl.pallas_call(
        kernel,
        in_specs=in_specs,
        out_specs=out_spec,
        out_shape=out,
        scratch_shapes=scratch,
        input_output_aliases=aliases,
        compiler_params=pltpu.CompilerParams(vmem_limit_bytes=VMEM),
        cost_estimate=pl.CostEstimate(flops=1, bytes_accessed=1, transcendentals=0),
    )(*operands)


def products_kernel(sets, groups, spans, before, *refs):
    row_refs, unit_refs = refs[:sets], refs[sets : sets + groups * len(spans)]
    out, total = refs[-2:]
    for step, (a, b) in enumerate(spans):
        units = jnp.concatenate(
            [ref[:, : b - a] for ref in unit_refs[step * groups : (step + 1) * groups]], axis=0
        )
        rows = jnp.concatenate([ref[:, a:b] for ref in row_refs], axis=0)
        value = lax.dot_general(
            units, rows, (((1,), (1,)), ((), ())), preferred_element_type=jnp.float32
        )
        if step > 0:
            value += total[...]
        elif before:
            value += refs[-3][...]
        if step < len(spans) - 1:
            total[...] = value
        else:
            out[...] = value.astype(out.dtype)


WHOLE = pl.BlockSpec(memory_space=pltpu.VMEM)


def products(row_sets, unit_sets, spans, before=None, out_type=jnp.bfloat16):
    groups = len(unit_sets) // len(spans)
    shape = (sum(u.shape[0] for u in unit_sets[:groups]), sum(r.shape[0] for r in row_sets))
    operands = (*row_sets, *unit_sets)
    if before is not None:
        operands += (before,)
    return call(
        functools.partial(
            products_kernel, len(row_sets), groups, tuple(spans), before is not None
        ),
        operands,
        [WHOLE] * len(operands),
        jax.ShapeDtypeStruct(shape, out_type),
        WHOLE,
        [pltpu.VMEM(shape, jnp.float32)],
        {},
    )


def activation_kernel(turned, side_ref, *refs):
    terms, outs = refs[:-2], refs[-2:]
    rows, units = outs[0].shape
    total = terms[0][...].astype(jnp.float32)
    for ref in terms[1:]:
        total += ref[...].astype(jnp.float32)
    gate, up = total[:units], total[units:]
    if turned:
        first = side_ref[0] == 0
        gate, up = jnp.where(first, gate, up), jnp.where(first, up, gate)
    hidden = (gate / (1.0 + jnp.exp(-gate)) * up).T
    for i, out in enumerate(outs):
        out[...] = hidden[i * rows : (i + 1) * rows].astype(out.dtype)


def activated(side, value, others, turned):
    operands = [side, value, *others]
    shape = (value.shape[1] // 2, value.shape[0] // 2)
    return call(
        functools.partial(activation_kernel, turned),
        operands,
        [pl.BlockSpec(memory_space=pltpu.SMEM)] + [WHOLE] * (len(operands) - 1),
        [jax.ShapeDtypeStruct(shape, jnp.bfloat16)] * 2,
        [WHOLE] * 2,
        [],
        {},
    )


def blocks_of(parts):
    found = []
    for i, (a, lanes, half, others) in enumerate(parts):
        for lane in range(0, lanes, 256):
            size = min(256, lanes - lane)
            fixed = a + lane + (half if others else 0)
            found.append((i, lane, size, (fixed, -half if others else half)))
    return found


def columns_of(side_ref, parts):
    side, at = side_ref[0], 0
    for i, lane, size, (fixed, turn) in blocks_of(parts):
        column = pl.ds(pl.multiple_of(fixed + side * turn, 128), size)
        yield pl.ds(at, size), i, slice(lane, lane + size), column
        at += size


def terms_sum(total, terms):
    for rows, weight in terms:
        term = jnp.dot(rows[...], weight, preferred_element_type=jnp.float32)
        total = term if total is None else total + term
    return total


def own_part_kernel(parts, side_ref, *refs):
    hidden, down, outs = refs[:2], refs[2:4], refs[4:]
    for _, i, lanes, column in columns_of(side_ref, parts):
        outs[i][:, lanes] = terms_sum(
            None, [(rows, ref[:, column]) for rows, ref in zip(hidden, down)]
        )


def own_parts(parts, side, hidden, down):
    return call(
        functools.partial(own_part_kernel, parts),
        [side, *hidden, *down],
        [pl.BlockSpec(memory_space=pltpu.SMEM)] + [WHOLE] * 4,
        [jax.ShapeDtypeStruct((hidden[0].shape[0], part[1]), jnp.float32) for part in parts],
        [WHOLE] * len(parts),
        [],
        {},
    )


def output_kernel(parts, known, side_ref, *refs):
    near = 1 if known else 4
    arrived = refs[2 : 2 + 2 * len(parts)]
    given = refs[2 + 2 * len(parts) : 2 + 2 * len(parts) + near]
    out, result, sems = refs[-3:]
    stores = []
    for n, (spot, i, lanes, column) in enumerate(columns_of(side_ref, parts)):
        terms = [(refs[m], arrived[2 * i + m][:, lanes]) for m in range(2)]
        if known:
            total = terms_sum(given[0][:, lanes], terms)
        else:
            total = terms_sum(None, [(given[m], given[2 + m][:, column]) for m in range(2)] + terms)
        result[:, spot] = total.astype(result.dtype)
        stores.append(
            pltpu.make_async_copy(result.at[:, spot], out.at[:, column], sems.at[n])
        )
        stores[-1].start()
    for copy in stores:
        copy.wait()


def output_part(result, parts, side, there, arrived, given, width):
    rows = there[0].shape[0]
    lanes = sum(part[1] for part in parts)
    operands = [side, *there, *arrived, *given]
    in_specs = [pl.BlockSpec(memory_space=pltpu.SMEM)] + [WHOLE] * (len(operands) - 1)
    aliases = {}
    if result is not None:
        aliases = {len(operands): 0}
        operands.append(result)
        in_specs.append(ANY)
    return call(
        functools.partial(output_kernel, parts, len(given) == 1),
        operands,
        in_specs,
        jax.ShapeDtypeStruct((rows, width), jnp.bfloat16),
        ANY,
        [
            pltpu.VMEM((rows, lanes), jnp.bfloat16),
            pltpu.SemaphoreType.DMA((len(blocks_of(parts)),)),
        ],
        aliases,
    )


def over_slices(partial_value):
    return [
        shifted(partial_value, "tensor", distance)
        for distance in range(1, lax.axis_size("tensor"))
    ]


def on_device(tokens, gate_weight, up_weight, down_weight):
    units, width = gate_weight.shape
    group = lax.axis_index("groups").astype(jnp.int32)
    first = group == 0
    side = group.reshape(1)

    spans = cuts(width, 128, FEATURE_SHARES)
    lane_cuts = [(2 * a, 2 * b) for a, b in cuts(width // 2, 128, LANE_SHARES)]
    count = len(spans)
    total_count = count + len(lane_cuts)
    relayed = total_count - WHOLES

    def piece(i, *after):
        if i < count:
            a, b = spans[i]
            gate, up = gate_weight, up_weight
            if after:
                gate, up = lax.optimization_barrier((gate, up, *after))[:2]
            return jnp.where(first, gate[:, a:b], up[:, a:b])
        a, b = lane_cuts[i - count]
        mid = (a + b) // 2
        down = tied(down_weight, *after)
        if i >= relayed:
            return down[:, a:b]
        return jnp.where(first, down[:, a:mid], down[:, mid:b])

    pieces = [piece(0), piece(1)]
    pieces += [piece(i, pieces[1]) for i in range(2, total_count)]
    waiting = [shifted(pieces[i], "dp", 1) for i in range(QUEUE)]
    landed, crossed, mates, crossed_mates = [], {}, {}, {}

    def advance(*after):
        i = len(landed)
        held = [*after, *landed[-1:]]
        held += [crossed[j] for j in range(count) if j + SWAP_WAIT == i]
        block = tied(waiting[i], *held)
        landed.append(block)
        if i < relayed:
            crossed[i] = across(block)
        if i + QUEUE < total_count:
            waiting.append(shifted(tied(pieces[i + QUEUE], block), "dp", 1))
        return block

    def pass_own(n, *after):
        mates[count + n] = mate(tied(landed[count + n], *after))

    def pass_other(n, *after):
        crossed_mates[count + n] = mate(tied(crossed[count + n], *after))

    def batch(lo, hi, now, before=None):
        held = [block for i in range(lo, hi) for block in (landed[i], crossed[i])]
        held = lax.optimization_barrier((*held, now))[:-1]
        kind = jnp.bfloat16 if hi == count else jnp.float32
        return products([tokens, tokens_mate], held, spans[lo:hi], before, kind)

    tokens_mate = mate(tied(tokens, pieces[0]))
    down_mate = mate(tied(down_weight, pieces[1]))
    due = {0: pieces[2:], OWN: [tokens_mate, down_mate]}
    value = own_value = None
    for i in range(relayed):
        now = advance(*due.get(i, []))
        after = due.setdefault(i + 1, [])
        if i == OWN:
            own_value = products(
                [tied(tokens, now), tokens_mate], [gate_weight, up_weight], [(0, width)]
            )
            own_sent = over_slices(own_value)
            after.append(own_value)
        if i == OWN_SUM:
            here, given = activated(
                side, own_value, [tied(block, now) for block in own_sent], False
            )
            here_mate = mate(given)
            after.append(here)
            due.setdefault(OWN_MATE, []).append(here_mate)
        for stage, lo, hi in BATCHES:
            if i == stage:
                value = batch(lo, hi, now, value)
                after.append(value)
                if hi == count:
                    sent = over_slices(value)
        if i == PASS[0]:
            pass_own(0, now)
        if i == PASS[1]:
            pass_other(0, now)
    there, given = activated(side, value, [tied(block, now) for block in sent], True)
    there_mate = mate(given)

    ready = {}

    def part_of(mark):
        n = mark if mark >= 0 else -1 - mark
        a, b = lane_cuts[n]
        half = (b - a) // 2
        if count + n >= relayed:
            return a, b - a, 0, False
        return a, half, half, mark < 0

    def write(result, *which):
        arrived = []
        for mark in which:
            if mark < 0:
                arrived += [crossed[count - 1 - mark], crossed_mates[count - 1 - mark]]
            else:
                arrived += [landed[count + mark], mates[count + mark]]
        given = [here, here_mate, down_weight, down_mate]
        if which[0] in ready:
            given = [ready[which[0]]]
        return output_part(
            result,
            tuple(part_of(mark) for mark in which),
            side,
            [there, there_mate],
            arrived,
            given,
            width,
        )

    result = None
    for step in TAIL:
        kind, numbers = step[0], step[1:]
        if kind == "own":
            for n in numbers:
                pass_own(n, now, *([] if result is None else [result]))
        elif kind == "other":
            for n in numbers:
                pass_other(n, now, *([] if result is None else [result]))
        elif kind == "write":
            result = write(result, *numbers)
        elif kind == "ready":
            found = own_parts(
                tuple(part_of(mark) for mark in numbers),
                side,
                [here, tied(here_mate, result)],
                [down_weight, down_mate],
            )
            ready.update(zip(numbers, found))
        elif kind == "last":
            held = [] if result is None else [result]
            held += ready.values()
            held += [crossed[count + n] for n in numbers]
            now = advance(*held)
            pass_own(len(landed) - 1 - count, now)
    return result


def solution(mesh):
    return jax.shard_map(
        on_device,
        mesh=mesh,
        in_specs=(
            P(("groups", "dp", "sub"), "tensor"),
            P(("dp", "sub"), "tensor"),
            P(("dp", "sub"), "tensor"),
            P(("dp", "sub"), "tensor"),
        ),
        out_specs=P(("groups", "dp", "sub"), "tensor"),
        check_vma=False,
    )
```
